512 devices in a mesh: blk: 128 (over z, y, core), kv: 4 (over x).
Axes of the slice: x: 4, y: 4, z: 16, core: 2. Of those that a mesh axis runs over, the one named last changes fastest.
Arguments:
- queries: bfloat16 [2048, 64, 128], P('blk', 'kv'), may hold values from -9 to 9
- prefix_keys: bfloat16 [128, 1024, 8, 128], P('blk', None, 'kv'), may hold values from -6 to 6
- prefix_values: bfloat16 [128, 1024, 8, 128], P('blk', None, 'kv'), may hold values from -6 to 6
- suffix_keys: bfloat16 [2048, 128, 8, 128], P('blk', None, 'kv'), may hold values from -6 to 6
- suffix_values: bfloat16 [2048, 128, 8, 128], P('blk', None, 'kv'), may hold values from -6 to 6
- out_weight: bfloat16 [8192, 8192], P('kv', 'blk'), may hold values from -0.25 to 0.25
- prefix_lists: int32 [2048, 8], P('blk'), may hold values from 0 to 127, all different within a row; in each aligned block of 16 rows (0 to 15, 16 to 31, ...) at most 2 rows name the same one
- suffix_lengths: int32 [2048], P('blk'), may hold values from 1 to 128, 163840 in all
- block_place: int32 [128], replicated, may hold values from 0 to 127, each once
Outputs:
- layer_out: bfloat16 [2048, 8192], P(None, ('blk', 'kv'))
The draws below stay inside these ranges and needn't reach their ends.
Inputs may be any that keep to these rules, and one draw needn't show every extreme that they name: `prefix_lists`: each row names 8 different blocks. Among the rows of one device no block is named more than 2 times, and in some device some block is named exactly 2 times. `suffix_lengths`: the largest is exactly 128. `block_place`: each stored position appears once.
All inputs are finite; a program needn't handle non-finite values. No bound on the sum of `suffix_lengths` on one device may be relied on, other than what follows from the above.
Results may differ from the reference program's by a relative error of at most 0.0058.
Values may be sent and summed in bfloat16 or wider, within the bound.
No kernel may reach another device: no remote copies, remote signals or barrier semaphores. Data moves between devices by JAX's collectives and lax.ppermute only.
A program may use at most 64 MiB of HBM per device.

```python
import math
import jax
import jax.numpy as jnp
import numpy as np
from jax import lax

D = 8192
HQ = 64
KVH = 8
HD = 128
REQ_DEV = 16
LIST = 8
BLOCK_LEN = 1024
SUF = 128
PREFIX_BLOCKS = 128
REQUESTS = 2048
CAP = 2


def draw_queries(key, part):
    key = jax.random.fold_in(key, 11)
    shape = (REQUESTS, HQ, HD)
    result = jnp.clip(2.5 * jax.random.normal(key, shape, jnp.float32), -9.0, 9.0)
    return result.astype(jnp.bfloat16)


def draw_prefix_keys(key, part):
    key = jax.random.fold_in(key, 12)
    shape = (PREFIX_BLOCKS, BLOCK_LEN, KVH, HD)
    result = jnp.clip(jax.random.normal(key, shape, jnp.float32), -6.0, 6.0)
    return result.astype(jnp.bfloat16)


def draw_suffix_keys(key, part):
    key = jax.random.fold_in(key, 13)
    shape = (REQUESTS, SUF, KVH, HD)
    result = jnp.clip(jax.random.normal(key, shape, jnp.float32), -6.0, 6.0)
    return result.astype(jnp.bfloat16)


def spiked(entries, key, source, target, parts, factor):
    owner, partner = [(jnp.arange(entries.shape[axis_at]) // (entries.shape[axis_at] // parts)).reshape([-1 if axis == axis_at else 1 for axis in range(entries.ndim)]) for axis_at in (source, target)]
    chosen = jax.random.permutation(key, parts)[partner]
    strong = (owner == chosen) | (owner == (partner + parts // 2) % parts)
    return jnp.where(strong, factor * entries, entries)


def block_levels(key, dims, shards, least, largest):
    gain = 1.0
    for dim, shards_of in shards:
        steps = jax.random.uniform(jax.random.fold_in(jax.random.fold_in(key, 6), dim), (shards_of,), jnp.float32, least / len(shards), largest / len(shards))
        gain = gain * jnp.repeat(jnp.exp(steps), dims[dim] // shards_of).reshape((-1,) + (1,) * (len(dims) - 1 - dim))
    return gain


def split_up(number_of, total, most, skew):
    weights = [(1 << 20) // math.isqrt(rank ** skew) + 1 for rank in range(2, number_of + 1)]
    surplus, holding = total - most - (number_of - 1), [1] * (number_of - 1)
    while surplus > 0:
        candidates = [i for i in range(number_of - 1) if holding[i] < most]
        whole, remaining = sum([weights[i] for i in candidates]), surplus
        for i in candidates:
            more = min(most - holding[i], max(1, remaining * weights[i] // whole), surplus)
            holding[i] = holding[i] + more
            surplus = surplus - more
    return np.array([most] + holding)


def uneven(stream_key, count, total, reach, skew):
    if count == 2:
        one = jax.random.randint(stream_key, (), max(1, total - reach), min(reach, total - 1) + 1)
        return jnp.stack([one, total - one])
    sizes = jnp.asarray(split_up(count, total, reach, skew), jnp.int32)
    pairs = (count - 1) // 2
    giver, sink = sizes[1:1 + 2 * pairs:2], sizes[2:2 + 2 * pairs:2]
    room = jnp.minimum(giver - 1, reach - sink)
    moved = jax.random.randint(jax.random.fold_in(stream_key, 1), (pairs,), 0, 1 << 20) % (room + 1)
    sizes = sizes.at[1:1 + 2 * pairs:2].set(giver - moved).at[2:2 + 2 * pairs:2].set(sink + moved)
    return sizes[jax.random.permutation(jax.random.fold_in(stream_key, 2), count)]


def routed_block(rng, own, number, rows, amount, top, bound, slope):
    sequence = jax.random.permutation(rng, amount)
    packed, common = load_shares(amount, rows * top, bound, slope, True), load_shares(amount, rows * top, bound, slope, False)
    places = jnp.arange(amount)

    def named(lengths, rotation):
        used = int((lengths > 0).sum())
        fixed = max(1, used // 4)
        moved = fixed + (places - fixed + rotation * (used - fixed)) % max(1, amount - fixed)
        return jnp.zeros((amount,), jnp.int32).at[sequence[jnp.where(places < fixed, places, moved)]].set(jnp.asarray(lengths, jnp.int32))

    lengths = jnp.where(number % 4 == 0, named(packed, number // 4), named(common, number - number // 4 - 1))
    mixed = jax.random.permutation(jax.random.fold_in(own, 3), amount)
    source_of, sink = mixed[0:amount // 2 * 2:2], mixed[1:amount // 2 * 2:2]
    room = jnp.minimum(lengths[source_of] - 1, bound - lengths[sink]) // 2
    room = jnp.where((source_of == sequence[0]) | (sink == sequence[0]) | (lengths[sink] == 0), 0, jnp.maximum(room, 0))
    moved = jax.random.randint(jax.random.fold_in(own, 4), (amount // 2,), 0, 1 << 20) % (room + 1)
    lengths = lengths.at[source_of].add(-moved).at[sink].add(moved)
    labels = jnp.searchsorted(jnp.cumsum(lengths), jnp.arange(rows * top), side="right").astype(jnp.int32)
    grid = labels.reshape(top, rows).T
    grid = grid[jax.random.permutation(jax.random.fold_in(own, 1), rows)]
    rotation = jax.random.randint(jax.random.fold_in(own, 2), (rows, 1), 0, top)
    return jnp.take_along_axis(grid, (jnp.arange(top)[None, :] + rotation) % top, axis=1)


def load_shares(number_of, total, limit, skew, full):
    portions = [(1 << 20) // math.isqrt(grade ** skew) + 1 for grade in range(1, number_of + 1)]
    largest = limit if full else min(limit, max(-(-total // number_of), total * portions[0] // sum(portions)))
    least = 1 if total - largest >= number_of - 1 else 0
    holding, rest = [largest] + [least] * (number_of - 1), total - largest - least * (number_of - 1)
    while rest > 0:
        movable = [i for i in range(1, number_of) if holding[i] < largest] or [i for i in range(1, number_of) if holding[i] < limit]
        pool, remaining = sum([portions[i] for i in movable]), rest
        for i in movable:
            addition = min(limit - holding[i], max(1, remaining * portions[i] // pool), rest)
            holding[i] = holding[i] + addition
            rest = rest - addition
    return np.array(holding)


def normal_values(key, dims, deviation, bound, pieces=(), held_as=jnp.bfloat16):
    array = jax.random.normal(key, dims, jnp.float32) * deviation
    if len(pieces) > 0:
        array = block_levels(key, dims, pieces, -0.22, 0.18) * array
    return jnp.clip(array, min=-bound, max=bound).astype(held_as)


def bell_draw_with(stream_key, shape, width, reach, pieces, heavy, held_as=jnp.bfloat16):
    array = width * jax.random.normal(stream_key, shape, jnp.float32)
    if pieces:
        array = array * block_levels(stream_key, shape, pieces, -0.22, 0.18)
    return jnp.clip(spiked(array, jax.random.fold_in(stream_key, 3), *heavy), -reach, reach).astype(held_as)


def setup_inputs(seed: int = 0) -> dict:
    keys = jax.random.split(jax.random.key(seed), 10)
    queries = draw_queries(jax.random.fold_in(keys[9], 71), 0)
    prefix_keys = draw_prefix_keys(jax.random.fold_in(keys[9], 71), 0)
    prefix_values = normal_values(keys[2], (PREFIX_BLOCKS, BLOCK_LEN, KVH, HD), 1.0, 6.0, ((0, 128), (2, 4)))
    suffix_keys = draw_suffix_keys(jax.random.fold_in(keys[9], 71), 0)
    suffix_values = normal_values(keys[4], (REQUESTS, SUF, KVH, HD), 1.0, 6.0, ((0, 128), (2, 4)))
    out_weight = bell_draw_with(keys[5], (HQ * HD, D), (HQ * HD) ** -0.5, 0.25, ((0, 4), (1, 128)), (0, 1, 128, 5.5))
    prefix_lists_keys = jax.random.split(jax.random.fold_in(keys[6], 1), REQUESTS // REQ_DEV)
    prefix_lists_turns = jax.random.permutation(jax.random.fold_in(keys[6], 3), REQUESTS // REQ_DEV)
    prefix_lists = jax.vmap(lambda own, number: routed_block(jax.random.fold_in(keys[6], 2), own, number, REQ_DEV, PREFIX_BLOCKS, LIST, CAP, 2))(prefix_lists_keys, prefix_lists_turns).reshape((REQUESTS, LIST))
    suffix_lengths = uneven(keys[7], REQUESTS, REQUESTS * SUF * 5 // 8, SUF, 1).astype(jnp.int32)
    block_place = jax.random.permutation(keys[8], PREFIX_BLOCKS).astype(jnp.int32)
    return {"queries": queries, "prefix_keys": prefix_keys, "prefix_values": prefix_values, "suffix_keys": suffix_keys, "suffix_values": suffix_values, "out_weight": out_weight, "prefix_lists": prefix_lists, "suffix_lengths": suffix_lengths, "block_place": block_place}


def partial_attention(one_query, block_keys, block_values, visible):
    kv_heads = block_keys.shape[1]
    grouped = one_query.astype(jnp.float32).reshape(kv_heads, HQ // kv_heads, HD)
    scores = jnp.einsum("hgd,lhd->hgl", grouped, block_keys.astype(jnp.float32), precision=lax.Precision.HIGHEST) * (HD ** -0.5)
    scores = jnp.where(visible[None, None, :], scores, jnp.float32(-1e30))
    row_top = jnp.max(scores, axis=-1)
    exponent = jnp.exp(scores - row_top[..., None])
    row_total = jnp.sum(exponent, axis=-1)
    weights = lax.optimization_barrier(exponent.astype(jnp.bfloat16)).astype(jnp.float32)
    mixed_out = jnp.einsum("hgl,lhd->hgd", weights, block_values.astype(jnp.float32), precision=lax.Precision.HIGHEST) / row_total[..., None]
    return mixed_out.reshape(HQ, HD), (row_top + jnp.log(row_total)).reshape(HQ)


def reference(queries, prefix_keys, prefix_values, suffix_keys, suffix_values, out_weight, prefix_lists, suffix_lengths, block_place):
    def one_request(operands):
        one_query, listed, length, own_keys, own_values = operands
        places = block_place[listed]

        def per_block(place):
            mixed_out, log_total = partial_attention(one_query, prefix_keys[place], prefix_values[place], jnp.ones((BLOCK_LEN,), bool))
            return lax.optimization_barrier(mixed_out.astype(jnp.bfloat16)).astype(jnp.float32), log_total

        block_out, block_lse = lax.map(per_block, places)
        own_out, own_lse = partial_attention(one_query, own_keys, own_values, jnp.arange(SUF) < length)
        every_out = jnp.concatenate([block_out, own_out[None]], axis=0)
        every_lse = jnp.concatenate([block_lse, own_lse[None]], axis=0)
        joint_top = jnp.max(every_lse, axis=0)
        scaled = jnp.exp(every_lse - joint_top[None])
        joined = jnp.sum(scaled[..., None] * every_out, axis=0) / jnp.sum(scaled, axis=0)[..., None]
        return joined.astype(jnp.bfloat16)

    attended = lax.map(one_request, (queries, prefix_lists, suffix_lengths, suffix_keys, suffix_values))
    flat_rows = attended.reshape(REQUESTS, HQ * HD)
    return jnp.dot(flat_rows, out_weight, preferred_element_type=jnp.float32).astype(jnp.bfloat16)
```

```python
import jax
import jax.numpy as jnp
from jax import lax
from jax.experimental import pallas as pl
from jax.experimental.pallas import tpu as pltpu
from jax.sharding import Mesh, PartitionSpec as P

ZS, YS, CS, XS = 16, 4, 2, 4
PLANE = YS * CS
ROWS = 16
HEADS = 16
HD = 128
WIDE = HEADS * HD
PACK = WIDE + 128
POOL = ZS * ROWS
SLOTS = POOL
CAP = SLOTS // PLANE
TOKENS = 1024
FAR = -1e30
SCALE = HD ** -0.5
LOG2E = 1.4426950408889634
PARAMS = pltpu.CompilerParams(vmem_limit_bytes=40 * 1024 * 1024)


def lanes(shape):
    return lax.broadcasted_iota(jnp.int32, shape, len(shape) - 1)


def split_parts(value):
    high = value.astype(jnp.bfloat16).astype(jnp.float32)
    rest = value - high
    middle = rest.astype(jnp.bfloat16).astype(jnp.float32)
    low = (rest - middle).astype(jnp.bfloat16).astype(jnp.float32)
    return high + pltpu.roll(middle, 16, 1) + pltpu.roll(low, 32, 1)


def join_parts(packed):
    whole = packed + pltpu.roll(packed, 112, 1) + pltpu.roll(packed, 96, 1)
    return jnp.where(lanes(whole.shape) < HEADS, whole, 0.0)


def dispatch_kernel(logical_ref, pool_ref, out_ref, select_ref):
    listed = pool_ref[:, WIDE:].astype(jnp.float32)
    logical = logical_ref[0:1, :]
    hot = jnp.zeros((POOL, 128), jnp.float32)
    for item in range(8):
        hot = jnp.where(listed[:, item : item + 1] == logical, 1.0, hot)
    hot = hot.astype(jnp.bfloat16)
    row = lax.broadcasted_iota(jnp.int32, (POOL, POOL), 0)
    column = lax.broadcasted_iota(jnp.int32, (POOL, POOL), 1)
    earlier = jnp.where(row > column, 1.0, 0.0).astype(jnp.bfloat16)
    rank = jnp.dot(earlier, hot, preferred_element_type=jnp.float32).astype(jnp.bfloat16)
    owner = lax.broadcasted_iota(jnp.int32, (128, SLOTS), 0)
    slot = lax.broadcasted_iota(jnp.int32, (128, SLOTS), 1)
    spread = jnp.where(slot // CAP == owner, 1.0, 0.0).astype(jnp.bfloat16)
    hot_at = jnp.dot(hot, spread, preferred_element_type=jnp.float32)
    rank_at = jnp.dot(rank, spread, preferred_element_type=jnp.float32)
    wanted = (lanes((POOL, SLOTS)) % CAP).astype(jnp.float32)
    select = jnp.where((hot_at > 0.5) & (rank_at == wanted), 1.0, 0.0).astype(jnp.bfloat16)
    select_ref[...] = select
    out_ref[...] = lax.dot_general(
        select, pool_ref[:, :WIDE], (((0,), (0,)), ((), ())), preferred_element_type=jnp.float32
    ).astype(jnp.bfloat16)


def attend_kernel(q_ref, k_ref, v_ref, out_ref):
    logs = jnp.zeros((SLOTS, 128), jnp.float32)
    lane = lanes((SLOTS, 128))
    for head in range(HEADS):
        group = slice((head // 8) * HD, (head // 8 + 1) * HD)
        at = slice(head * HD, (head + 1) * HD)
        scores = lax.dot_general(
            q_ref[:, at], k_ref[:, group], (((1,), (1,)), ((), ())), preferred_element_type=jnp.float32
        )
        top = jnp.max(scores, axis=1, keepdims=True)
        grown = jnp.exp2((scores - top) * (SCALE * LOG2E))
        total = jnp.sum(grown, axis=1, keepdims=True)
        mixed = jnp.dot(
            grown.astype(jnp.bfloat16), v_ref[:, group], preferred_element_type=jnp.float32
        )
        out_ref[:, at] = (mixed / total).astype(jnp.bfloat16)
        logs = jnp.where(lane == head, top * SCALE + jnp.log(total), logs)
    flags = jnp.where((lane >= 48) & (lane < 64), 1.0, 0.0)
    out_ref[:, WIDE:] = (split_parts(logs) + flags).astype(jnp.bfloat16)


STAY, NEXT, BACK, NEXT2, BACK2 = (0, 4, 8, 12), (1, 5, 9, 13), (15, 3, 7, 11), (2, 6), (14, 10)


def gather_kernel(place_ref, back_ref, select_ref, *refs):
    outs, joined_ref = refs[:-1], refs[-1]
    select = select_ref[...]
    packed = back_ref[:, WIDE:]
    lane = lanes((POOL, 128))
    slot = lanes((POOL, SLOTS))
    tops = []
    hots = []
    for block in range(PLANE):
        part = jnp.where(slot // CAP == block, select, jnp.zeros_like(select))
        found = jnp.dot(part, packed, preferred_element_type=jnp.float32)
        hot = pltpu.roll(found, 80, 1)
        hot = (hot > 0.5) & (lane < HEADS)
        tops.append(jnp.where(hot, join_parts(found), FAR))
        hots.append(hot)
    top = tops[0]
    for other in tops[1:]:
        top = jnp.maximum(top, other)
    total = jnp.zeros((POOL, 128), jnp.float32)
    for log, hot in zip(tops, hots):
        total = total + jnp.where(hot, jnp.exp(log - top), 0.0)
    whole = jnp.where(lane < HEADS, top + jnp.log(jnp.maximum(total, 1.0)), 0.0)
    whole_parts = split_parts(whole).astype(jnp.bfloat16)
    at_slot = lax.dot_general(
        select, whole_parts, (((0,), (0,)), ((), ())), preferred_element_type=jnp.float32
    )
    weight = jnp.exp(join_parts(packed.astype(jnp.float32)) - join_parts(at_slot))
    for head in range(HEADS):
        at = slice(head * HD, (head + 1) * HD)
        scaled = weight[:, head : head + 1] * back_ref[:, at].astype(jnp.float32)
        high = scaled.astype(jnp.bfloat16)
        low = (scaled - high.astype(jnp.float32)).astype(jnp.bfloat16)
        joined_ref[:, at] = (
            jnp.dot(select, high, preferred_element_type=jnp.float32)
            + jnp.dot(select, low, preferred_element_type=jnp.float32)
        ).astype(jnp.bfloat16)
    joined_ref[:, WIDE:] = whole_parts
    place = place_ref[0]
    for out_ref, distances in zip(outs, (STAY, NEXT, BACK, NEXT2, BACK2)):
        for index, distance in enumerate(distances):
            block = lax.rem(place + distance, ZS)
            start = pl.multiple_of(block * ROWS, ROWS)
            out_ref[index * ROWS : (index + 1) * ROWS, :] = joined_ref[pl.ds(start, ROWS), :]


def merge(terms):
    top = terms[0][1]
    for _, log in terms[1:]:
        top = jnp.maximum(top, log)
    lane = lanes((ROWS, 128))
    weights = [jnp.exp(log - top) for _, log in terms]
    total = weights[0]
    for weight in weights[1:]:
        total = total + weight
    columns = []
    for head in range(HEADS):
        at = slice(head * HD, (head + 1) * HD)
        row = None
        for (rows, _), weight in zip(terms, weights):
            term = weight[:, head : head + 1] * rows(at)
            row = term if row is None else row + term
        columns.append(row / total[:, head : head + 1])
    return columns, jnp.where(lane < HEADS, top + jnp.log(total), 0.0)


def packed_term(ref, index):
    rows = slice(index * ROWS, (index + 1) * ROWS)
    return (
        lambda at: ref[rows, at].astype(jnp.float32),
        join_parts(ref[rows, WIDE:].astype(jnp.float32)),
    )


def middle_kernel(stay_ref, next_ref, back_ref, next2_ref, back2_ref, *outs):
    for quarter, out_ref in enumerate(outs):
        terms = [packed_term(stay_ref, quarter), packed_term(next_ref, quarter), packed_term(back_ref, quarter)]
        if quarter < 2:
            terms.append(packed_term(next2_ref, quarter))
        if quarter in (0, 3):
            terms.append(packed_term(back2_ref, 0 if quarter == 0 else 1))
        columns, log = merge(terms)
        for head in range(HEADS):
            out_ref[:, head * HD : (head + 1) * HD] = columns[head].astype(jnp.bfloat16)
        out_ref[:, WIDE:] = split_parts(log).astype(jnp.bfloat16)


def final_kernel(a_ref, b_ref, c_ref, d_ref, own_ref, own_log_ref, out_ref):
    terms = [packed_term(ref, 0) for ref in (a_ref, b_ref, c_ref, d_ref)]
    terms.append((lambda at: own_ref[:, at], own_log_ref[...]))
    columns, _ = merge(terms)
    for head in range(HEADS):
        out_ref[:, head * HD : (head + 1) * HD] = columns[head].astype(jnp.bfloat16)


def own_partials(queries, own_keys, own_values, lengths):
    req_rows, q_heads, head_dim = queries.shape
    kv_heads = own_keys.shape[2]
    grouped = queries.reshape(req_rows, kv_heads, q_heads // kv_heads, head_dim)
    scores = jnp.einsum(
        "rhgd,rlhd->rhgl", grouped, own_keys, preferred_element_type=jnp.float32
    ) * head_dim ** (-0.5)
    visible = jnp.arange(own_keys.shape[1])[None, None, None, :] < lengths[:, None, None, None]
    scores = jnp.where(visible, scores, jnp.float32(-1e30))
    row_top = jnp.max(scores, axis=-1)
    exponent = jnp.exp(scores - row_top[..., None])
    row_total = jnp.sum(exponent, axis=-1)
    weights = exponent.astype(jnp.bfloat16)
    mixed_out = (
        jnp.einsum("rhgl,rlhd->rhgd", weights, own_values, preferred_element_type=jnp.float32)
        / row_total[..., None]
    )
    return (
        mixed_out.reshape(req_rows, q_heads * head_dim),
        (row_top + jnp.log(row_total)).reshape(req_rows, q_heads),
    )


def packed(rows):
    return jax.ShapeDtypeStruct((rows, PACK), jnp.bfloat16)


def shifted(value, distance):
    return lax.ppermute(value, "z", [(place, (place + distance) % ZS) for place in range(ZS)])


def on_device(
    queries,
    prefix_keys,
    prefix_values,
    suffix_keys,
    suffix_values,
    out_weight,
    prefix_lists,
    suffix_lengths,
    block_place,
):
    place = lax.axis_index("z")
    flat_queries = queries.reshape(ROWS, WIDE)
    listed = jnp.pad(prefix_lists.astype(jnp.bfloat16), ((0, 0), (0, 120)))
    pool = lax.all_gather(
        jnp.concatenate([flat_queries, listed], axis=1), "z", axis=0, tiled=True
    )

    stored = place * PLANE + jnp.arange(128)
    here = (block_place[None, :] == stored[:, None]) & (jnp.arange(128) < PLANE)[:, None]
    logical = jnp.sum(jnp.where(here, jnp.arange(128)[None, :], 0), axis=1)
    logical = jnp.where(jnp.arange(128) < PLANE, logical, -1).astype(jnp.float32)

    outgoing, select = pl.pallas_call(
        dispatch_kernel,
        out_shape=(
            jax.ShapeDtypeStruct((SLOTS, WIDE), jnp.bfloat16),
            jax.ShapeDtypeStruct((POOL, SLOTS), jnp.bfloat16),
        ),
        compiler_params=PARAMS,
        name="dispatch",
    )(jnp.broadcast_to(logical[None], (8, 128)), pool)

    turned, pool_seen = lax.optimization_barrier((out_weight.T, pool))
    plane_weight = lax.all_gather(turned, ("y", "c"), axis=0, tiled=True)

    arrived = lax.all_to_all(outgoing, ("y", "c"), split_axis=0, concat_axis=0, tiled=True)
    partials = pl.pallas_call(
        attend_kernel, out_shape=packed(SLOTS), compiler_params=PARAMS, name="attend"
    )(
        arrived,
        prefix_keys.reshape(TOKENS, 2 * HD),
        prefix_values.reshape(TOKENS, 2 * HD),
    )
    back = lax.all_to_all(partials, ("y", "c"), split_axis=0, concat_axis=0, tiled=True)
    stay, near, rear, near2, rear2 = pl.pallas_call(
        gather_kernel,
        in_specs=[
            pl.BlockSpec(memory_space=pltpu.SMEM),
            pl.BlockSpec(memory_space=pltpu.VMEM),
            pl.BlockSpec(memory_space=pltpu.VMEM),
        ],
        out_shape=(packed(64), packed(64), packed(64), packed(32), packed(32)),
        scratch_shapes=[pltpu.VMEM((POOL, PACK), jnp.bfloat16)],
        compiler_params=PARAMS,
        name="gather",
    )(place.reshape(1).astype(jnp.int32), back, select)
    near, rear = shifted(near, 1), shifted(rear, -1)
    near2, rear2 = shifted(near2, 2), shifted(rear2, -2)
    kept, plus4, plus8, minus4 = pl.pallas_call(
        middle_kernel,
        out_shape=(packed(ROWS),) * 4,
        compiler_params=PARAMS,
        name="middle",
    )(stay, near, rear, near2, rear2)
    plus4, minus4, plus8 = shifted(plus4, 4), shifted(minus4, -4), shifted(plus8, 8)

    own_out, own_log = own_partials(queries, suffix_keys, suffix_values, suffix_lengths)
    attended = pl.pallas_call(
        final_kernel,
        out_shape=jax.ShapeDtypeStruct((ROWS, WIDE), jnp.bfloat16),
        compiler_params=PARAMS,
        name="final",
    )(kept, plus4, plus8, minus4, own_out, jnp.pad(own_log, ((0, 0), (0, 112))))

    rows = lax.all_gather(attended, "z", axis=0, tiled=True)
    terms = lax.dot_general(
        plane_weight, rows, (((1,), (1,)), ((), ())), preferred_element_type=jnp.float32
    )
    terms = lax.all_to_all(
        terms.reshape(PLANE * XS, 16, POOL),
        ("y", "c", "kv"),
        split_axis=0,
        concat_axis=0,
        tiled=True,
    )
    summed = jnp.sum(terms.reshape(PLANE, XS, 16, ZS, ROWS), axis=1).astype(jnp.bfloat16)
    return summed.transpose(2, 0, 3, 1).reshape(ZS * PLANE * ROWS, 16)


def solution(mesh):
    blk = ("z", "y", "c")
    fine = Mesh(mesh.devices.reshape(ZS, YS, CS, XS), blk + ("kv",))
    placed = (
        P(blk, "kv", None),
        P(blk, None, "kv", None),
        P(blk, None, "kv", None),
        P(blk, None, "kv", None),
        P(blk, None, "kv", None),
        P("kv", blk),
        P(blk, None),
        P(blk),
        P(),
    )
    return jax.shard_map(
        on_device, mesh=fine, in_specs=placed, out_specs=P(None, blk + ("kv",)), check_vma=False
    )
```

```python
import jax
import jax.numpy as jnp
from jax import lax
from jax.experimental import pallas as pl
from jax.experimental.pallas import tpu as pltpu
from jax.sharding import Mesh, PartitionSpec as P

ZH, ZP, ZQ, YS, CS, XS = 4, 2, 2, 4, 2, 4
QUAD = ZP * ZQ * YS * CS
GROUP = ZP * YS * CS
ROWS = 16
HEADS = 16
HD = 128
WIDE = HEADS * HD
PACK = WIDE + 128
POOL = ZH * ROWS
CAP = 2 * ZH
SLOTS = QUAD * CAP
TOKENS = 1024
FAR = -1e30
SCALE = HD ** -0.5
LOG2E = 1.4426950408889634
PARAMS = pltpu.CompilerParams(vmem_limit_bytes=40 * 1024 * 1024)


def lanes(shape):
    return lax.broadcasted_iota(jnp.int32, shape, len(shape) - 1)


def split_parts(value):
    high = value.astype(jnp.bfloat16).astype(jnp.float32)
    rest = value - high
    middle = rest.astype(jnp.bfloat16).astype(jnp.float32)
    low = (rest - middle).astype(jnp.bfloat16).astype(jnp.float32)
    return high + pltpu.roll(middle, 16, 1) + pltpu.roll(low, 32, 1)


def join_parts(packed):
    whole = packed + pltpu.roll(packed, 112, 1) + pltpu.roll(packed, 96, 1)
    return jnp.where(lanes(whole.shape) < HEADS, whole, 0.0)


def dispatch_kernel(logical_ref, pool_ref, out_ref, select_ref):
    listed = pool_ref[:, WIDE:].astype(jnp.float32)
    logical = logical_ref[0:1, :]
    hot = jnp.zeros((POOL, 128), jnp.float32)
    for item in range(8):
        hot = jnp.where(listed[:, item : item + 1] == logical, 1.0, hot)
    hot = hot.astype(jnp.bfloat16)
    row = lax.broadcasted_iota(jnp.int32, (POOL, POOL), 0)
    column = lax.broadcasted_iota(jnp.int32, (POOL, POOL), 1)
    earlier = jnp.where(row > column, 1.0, 0.0).astype(jnp.bfloat16)
    rank = jnp.dot(earlier, hot, preferred_element_type=jnp.float32).astype(jnp.bfloat16)
    owner = lax.broadcasted_iota(jnp.int32, (128, SLOTS), 0)
    slot = lax.broadcasted_iota(jnp.int32, (128, SLOTS), 1)
    spread = jnp.where(slot // CAP == owner, 1.0, 0.0).astype(jnp.bfloat16)
    hot_at = jnp.dot(hot, spread, preferred_element_type=jnp.float32)
    rank_at = jnp.dot(rank, spread, preferred_element_type=jnp.float32)
    wanted = (lanes((POOL, SLOTS)) % CAP).astype(jnp.float32)
    select = jnp.where((hot_at > 0.5) & (rank_at == wanted), 1.0, 0.0)
    select_ref[...] = select
    out_ref[...] = lax.dot_general(
        select.astype(jnp.bfloat16),
        pool_ref[:, :WIDE],
        (((0,), (0,)), ((), ())),
        preferred_element_type=jnp.float32,
    ).astype(jnp.bfloat16)


def attend_kernel(q_ref, k_ref, v_ref, weight_ref, out_ref):
    logs = jnp.zeros((SLOTS, 128), jnp.float32)
    lane = lanes((SLOTS, 128))
    for head in range(HEADS):
        group = slice((head // 8) * HD, (head // 8 + 1) * HD)
        at = slice(head * HD, (head + 1) * HD)
        scores = lax.dot_general(
            q_ref[:, at], k_ref[:, group], (((1,), (1,)), ((), ())), preferred_element_type=jnp.float32
        )
        top = jnp.max(scores, axis=1, keepdims=True)
        grown = jnp.exp2((scores - top) * (SCALE * LOG2E))
        total = jnp.sum(grown, axis=1, keepdims=True)
        mixed = jnp.dot(
            grown.astype(jnp.bfloat16), v_ref[:, group], preferred_element_type=jnp.float32
        )
        out_ref[:, at] = (mixed / total).astype(jnp.bfloat16)
        logs = jnp.where(lane == head, top * SCALE + jnp.log(total), logs)
    out_ref[:, WIDE:] = split_parts(logs).astype(jnp.bfloat16)


def gather_kernel(back_ref, select_ref, joined_ref):
    chosen = select_ref[...] > 0.5
    slot_logs = join_parts(back_ref[:, WIDE:].astype(jnp.float32)).T
    lane = lanes((POOL, 128))
    logs = jnp.zeros((POOL, 128), jnp.float32)
    for head in range(HEADS):
        at = slice(head * HD, (head + 1) * HD)
        log = jnp.where(chosen, slot_logs[head : head + 1, :], FAR)
        top = jnp.max(log, axis=1, keepdims=True)
        grown = jnp.where(chosen, jnp.exp(log - top), 0.0)
        total = jnp.maximum(jnp.sum(grown, axis=1, keepdims=True), 0.5)
        weight = grown / total
        high = weight.astype(jnp.bfloat16)
        low = (weight - high.astype(jnp.float32)).astype(jnp.bfloat16)
        mixed = jnp.dot(high, back_ref[:, at], preferred_element_type=jnp.float32)
        mixed = mixed + jnp.dot(low, back_ref[:, at], preferred_element_type=jnp.float32)
        joined_ref[:, at] = mixed.astype(jnp.bfloat16)
        logs = jnp.where(lane == head, top + jnp.log(total), logs)
    joined_ref[:, WIDE:] = split_parts(logs).astype(jnp.bfloat16)


def merge(terms):
    top = terms[0][1]
    for _, log in terms[1:]:
        top = jnp.maximum(top, log)
    lane = lanes((ROWS, 128))
    weights = [jnp.exp(log - top) for _, log in terms]
    total = weights[0]
    for weight in weights[1:]:
        total = total + weight
    columns = []
    for head in range(HEADS):
        at = slice(head * HD, (head + 1) * HD)
        row = None
        for (rows, _), weight in zip(terms, weights):
            term = weight[:, head : head + 1] * rows(at)
            row = term if row is None else row + term
        columns.append(row / total[:, head : head + 1])
    return columns, jnp.where(lane < HEADS, top + jnp.log(total), 0.0)


def packed_term(ref, index):
    rows = slice(index * ROWS, (index + 1) * ROWS)
    return (
        lambda at: ref[rows, at].astype(jnp.float32),
        join_parts(ref[rows, WIDE:].astype(jnp.float32)),
    )


def final_kernel(far_ref, own_ref, own_log_ref, out_ref):
    terms = [packed_term(far_ref, index) for index in range(ZH)]
    terms.append((lambda at: own_ref[:, at], own_log_ref[...]))
    columns, _ = merge(terms)
    for head in range(HEADS):
        out_ref[:, head * HD : (head + 1) * HD] = columns[head].astype(jnp.bfloat16)


def project_kernel(rows_ref, weight_ref, out_ref):
    terms = lax.dot_general(
        weight_ref[...], rows_ref[...], (((1,), (1,)), ((), ())), preferred_element_type=jnp.float32
    )
    owners = out_ref.shape[1]
    for owner in range(owners):
        for part in range(XS):
            first = (owner * XS + part) * 16
            out_ref[part, owner] = terms[first : first + 16, :]


def sum_kernel(place_ref, terms_ref, out_ref):
    place = place_ref[0]
    for owner in range(YS * CS):
        for half in range(ZP):
            index = owner * ZP + half
            term = terms_ref[0, index]
            for part in range(1, XS):
                term = term + terms_ref[part, index]
            side = place if half == 0 else 1 - place
            out_ref[side * (YS * CS) + owner] = term.astype(jnp.bfloat16)


def settle_kernel(place_ref, parts_ref, out_ref):
    place = place_ref[0]
    for group in range(GROUP):
        side, owner = divmod(group, YS * CS)
        turned = parts_ref[group].astype(jnp.float32).T.astype(jnp.bfloat16)
        for half in range(ZQ):
            near = place if half == 0 else 1 - place
            for far in range(ZH):
                start = ((far * ZP + side) * ZQ + near) * YS * CS + owner
                first = (half * ZH + far) * ROWS
                out_ref[pl.ds(pl.multiple_of(start * ROWS, ROWS), ROWS), :] = turned[
                    first : first + ROWS, :
                ]


def own_partials(queries, own_keys, own_values, lengths):
    req_rows, q_heads, head_dim = queries.shape
    kv_heads = own_keys.shape[2]
    grouped = queries.reshape(req_rows, kv_heads, q_heads // kv_heads, head_dim)
    scores = jnp.einsum(
        "rhgd,rlhd->rhgl", grouped, own_keys, preferred_element_type=jnp.float32
    ) * head_dim ** (-0.5)
    visible = jnp.arange(own_keys.shape[1])[None, None, None, :] < lengths[:, None, None, None]
    scores = jnp.where(visible, scores, jnp.float32(-1e30))
    row_top = jnp.max(scores, axis=-1)
    exponent = jnp.exp(scores - row_top[..., None])
    row_total = jnp.sum(exponent, axis=-1)
    weights = exponent.astype(jnp.bfloat16)
    mixed_out = (
        jnp.einsum("rhgl,rlhd->rhgd", weights, own_values, preferred_element_type=jnp.float32)
        / row_total[..., None]
    )
    return (
        mixed_out.reshape(req_rows, q_heads * head_dim),
        (row_top + jnp.log(row_total)).reshape(req_rows, q_heads),
    )


def packed(rows):
    return jax.ShapeDtypeStruct((rows, PACK), jnp.bfloat16)


def spread_along(value, axis, count):
    copies = jnp.broadcast_to(value[None], (count,) + value.shape)
    everyone = lax.all_to_all(copies, axis, split_axis=0, concat_axis=0, tiled=True)
    return everyone.reshape((count * value.shape[0],) + value.shape[1:])


def on_device(
    queries,
    prefix_keys,
    prefix_values,
    suffix_keys,
    suffix_values,
    out_weight,
    prefix_lists,
    suffix_lengths,
    block_place,
):
    quad = ("zp", "zq", "y", "c")
    swap = [(0, 1), (1, 0)]
    flat_queries = queries.reshape(ROWS, WIDE)
    listed = jnp.pad(prefix_lists.astype(jnp.bfloat16), ((0, 0), (0, 120)))
    pool = spread_along(jnp.concatenate([flat_queries, listed], axis=1), "zh", ZH)

    turned = out_weight.T
    turned = jnp.concatenate([turned, lax.ppermute(turned, "zp", swap)], axis=0)
    near_weight = lax.all_gather(turned, ("y", "c"), axis=0, tiled=True)

    lane = jnp.arange(128)
    stored = lax.axis_index("zh") * QUAD + lane
    here = (block_place[None, :] == stored[:, None]) & (lane < QUAD)[:, None]
    logical = jnp.sum(jnp.where(here, lane[None, :], 0), axis=1)
    logical = jnp.where(lane < QUAD, logical, -1).astype(jnp.float32)

    outgoing, select = pl.pallas_call(
        dispatch_kernel,
        out_shape=(
            jax.ShapeDtypeStruct((SLOTS, WIDE), jnp.bfloat16),
            jax.ShapeDtypeStruct((POOL, SLOTS), jnp.float32),
        ),
        compiler_params=PARAMS,
        name="dispatch",
    )(jnp.broadcast_to(logical[None], (8, 128)), pool)
    arrived = lax.all_to_all(outgoing, quad, split_axis=0, concat_axis=0, tiled=True)
    partials = pl.pallas_call(
        attend_kernel,
        in_specs=[pl.BlockSpec(memory_space=pltpu.VMEM)] * 3 + [pl.BlockSpec(memory_space=pl.ANY)],
        out_shape=packed(SLOTS),
        compiler_params=PARAMS,
        name="attend",
    )(
        arrived,
        prefix_keys.reshape(TOKENS, 2 * HD),
        prefix_values.reshape(TOKENS, 2 * HD),
        near_weight,
    )
    back = lax.all_to_all(partials, quad, split_axis=0, concat_axis=0, tiled=True)
    joined = pl.pallas_call(
        gather_kernel, out_shape=packed(POOL), compiler_params=PARAMS, name="gather"
    )(back, select)
    far = lax.all_to_all(joined, "zh", split_axis=0, concat_axis=0, tiled=True)

    own_out, own_log = own_partials(queries, suffix_keys, suffix_values, suffix_lengths)
    attended = pl.pallas_call(
        final_kernel,
        out_shape=jax.ShapeDtypeStruct((ROWS, WIDE), jnp.bfloat16),
        compiler_params=PARAMS,
        name="final",
    )(far, own_out, jnp.pad(own_log, ((0, 0), (0, 112))))

    rows = spread_along(attended, "zh", ZH)
    rows = jnp.concatenate([rows, lax.ppermute(rows, "zq", swap)], axis=0)
    steps = 4
    terms = pl.pallas_call(
        project_kernel,
        grid=(steps,),
        in_specs=[
            pl.BlockSpec((ZQ * POOL, WIDE), lambda step: (0, 0)),
            pl.BlockSpec((GROUP * 64 // steps, WIDE), lambda step: (step, 0)),
        ],
        out_specs=pl.BlockSpec((XS, GROUP // steps, 16, ZQ * POOL), lambda step: (0, step, 0, 0)),
        out_shape=jax.ShapeDtypeStruct((XS, GROUP, 16, ZQ * POOL), jnp.float32),
        compiler_params=PARAMS,
        name="project",
    )(rows, near_weight)
    terms = lax.all_to_all(terms, "kv", split_axis=0, concat_axis=0, tiled=True)
    one = [pl.BlockSpec(memory_space=pltpu.SMEM), pl.BlockSpec(memory_space=pltpu.VMEM)]
    parts = pl.pallas_call(
        sum_kernel,
        in_specs=one,
        out_shape=jax.ShapeDtypeStruct((GROUP, 16, ZQ * POOL), jnp.bfloat16),
        compiler_params=PARAMS,
        name="sum",
    )(lax.axis_index("zp").reshape(1).astype(jnp.int32), terms)
    parts = lax.all_to_all(parts, ("zp", "y", "c"), split_axis=0, concat_axis=0, tiled=True)
    return pl.pallas_call(
        settle_kernel,
        in_specs=one,
        out_shape=jax.ShapeDtypeStruct((ZH * QUAD * ROWS, 16), jnp.bfloat16),
        compiler_params=PARAMS,
        name="settle",
    )(lax.axis_index("zq").reshape(1).astype(jnp.int32), parts)


def solution(mesh):
    blk = ("zh", "zp", "zq", "y", "c")
    fine = Mesh(mesh.devices.reshape(ZH, ZP, ZQ, YS, CS, XS), blk + ("kv",))
    placed = (
        P(blk, "kv", None),
        P(blk, None, "kv", None),
        P(blk, None, "kv", None),
        P(blk, None, "kv", None),
        P(blk, None, "kv", None),
        P("kv", blk),
        P(blk, None),
        P(blk),
        P(),
    )
    return jax.shard_map(
        on_device, mesh=fine, in_specs=placed, out_specs=P(None, blk + ("kv",)), check_vma=False
    )
```

```python
import jax
import jax.numpy as jnp
from jax import lax
from jax.experimental import pallas as pl
from jax.experimental.pallas import tpu as pltpu
from jax.sharding import Mesh, PartitionSpec as P

ZH, ZP, ZQ, YS, CS, XS = 4, 2, 2, 4, 2, 4
QUAD = ZP * ZQ * YS * CS
GROUP = ZP * YS * CS
ROWS = 16
HEADS = 16
HD = 128
WIDE = HEADS * HD
PACK = WIDE + 128
POOL = ZH * ROWS
CAP = 2 * ZH
SLOTS = QUAD * CAP
TOKENS = 1024
FAR = -1e30
SCALE = HD ** -0.5
LOG2E = 1.4426950408889634
PARAMS = pltpu.CompilerParams(vmem_limit_bytes=40 * 1024 * 1024)


def lanes(shape):
    return lax.broadcasted_iota(jnp.int32, shape, len(shape) - 1)


def split_parts(value):
    high = value.astype(jnp.bfloat16).astype(jnp.float32)
    rest = value - high
    middle = rest.astype(jnp.bfloat16).astype(jnp.float32)
    low = (rest - middle).astype(jnp.bfloat16).astype(jnp.float32)
    return high + pltpu.roll(middle, 16, 1) + pltpu.roll(low, 32, 1)


def join_parts(packed):
    whole = packed + pltpu.roll(packed, 112, 1) + pltpu.roll(packed, 96, 1)
    return jnp.where(lanes(whole.shape) < HEADS, whole, 0.0)


def dispatch_kernel(logical_ref, pool_ref, sides_ref, out_ref, select_ref):
    listed = pool_ref[:, WIDE:].astype(jnp.float32)
    logical = logical_ref[0:1, :]
    hot = jnp.zeros((POOL, 128), jnp.float32)
    for item in range(8):
        hot = jnp.where(listed[:, item : item + 1] == logical, 1.0, hot)
    hot = hot.astype(jnp.bfloat16)
    row = lax.broadcasted_iota(jnp.int32, (POOL, POOL), 0)
    column = lax.broadcasted_iota(jnp.int32, (POOL, POOL), 1)
    earlier = jnp.where(row > column, 1.0, 0.0).astype(jnp.bfloat16)
    rank = jnp.dot(earlier, hot, preferred_element_type=jnp.float32).astype(jnp.bfloat16)
    owner = lax.broadcasted_iota(jnp.int32, (128, SLOTS), 0)
    slot = lax.broadcasted_iota(jnp.int32, (128, SLOTS), 1)
    spread = jnp.where(slot // CAP == owner, 1.0, 0.0).astype(jnp.bfloat16)
    hot_at = jnp.dot(hot, spread, preferred_element_type=jnp.float32)
    rank_at = jnp.dot(rank, spread, preferred_element_type=jnp.float32)
    wanted = (lanes((POOL, SLOTS)) % CAP).astype(jnp.float32)
    select = jnp.where((hot_at > 0.5) & (rank_at == wanted), 1.0, 0.0)
    select_ref[...] = select
    out_ref[...] = lax.dot_general(
        select.astype(jnp.bfloat16),
        pool_ref[:, :WIDE],
        (((0,), (0,)), ((), ())),
        preferred_element_type=jnp.float32,
    ).astype(jnp.bfloat16)


def attend_kernel(q_ref, k_ref, v_ref, above_ref, below_ref, out_ref):
    logs = jnp.zeros((SLOTS, 128), jnp.float32)
    lane = lanes((SLOTS, 128))
    for head in range(HEADS):
        group = slice((head // 8) * HD, (head // 8 + 1) * HD)
        at = slice(head * HD, (head + 1) * HD)
        scores = lax.dot_general(
            q_ref[:, at], k_ref[:, group], (((1,), (1,)), ((), ())), preferred_element_type=jnp.float32
        )
        top = jnp.max(scores, axis=1, keepdims=True)
        grown = jnp.exp2((scores - top) * (SCALE * LOG2E))
        total = jnp.sum(grown, axis=1, keepdims=True)
        mixed = jnp.dot(
            grown.astype(jnp.bfloat16), v_ref[:, group], preferred_element_type=jnp.float32
        )
        out_ref[:, at] = (mixed / total).astype(jnp.bfloat16)
        logs = jnp.where(lane == head, top * SCALE + jnp.log(total), logs)
    out_ref[:, WIDE:] = split_parts(logs).astype(jnp.bfloat16)


def gather_kernel(back_ref, select_ref, mine_ref, joined_ref):
    chosen = select_ref[...] > 0.5
    slot_logs = join_parts(back_ref[:, WIDE:].astype(jnp.float32)).T
    lane = lanes((POOL, 128))
    logs = jnp.zeros((POOL, 128), jnp.float32)
    for head in range(HEADS):
        at = slice(head * HD, (head + 1) * HD)
        log = jnp.where(chosen, slot_logs[head : head + 1, :], FAR)
        top = jnp.max(log, axis=1, keepdims=True)
        grown = jnp.where(chosen, jnp.exp(log - top), 0.0)
        total = jnp.maximum(jnp.sum(grown, axis=1, keepdims=True), 0.5)
        weight = grown / total
        high = weight.astype(jnp.bfloat16)
        low = (weight - high.astype(jnp.float32)).astype(jnp.bfloat16)
        mixed = jnp.dot(high, back_ref[:, at], preferred_element_type=jnp.float32)
        mixed = mixed + jnp.dot(low, back_ref[:, at], preferred_element_type=jnp.float32)
        joined_ref[:, at] = mixed.astype(jnp.bfloat16)
        logs = jnp.where(lane == head, top + jnp.log(total), logs)
    joined_ref[:, WIDE:] = split_parts(logs).astype(jnp.bfloat16)


def merge(terms):
    top = terms[0][1]
    for _, log in terms[1:]:
        top = jnp.maximum(top, log)
    lane = lanes((ROWS, 128))
    weights = [jnp.exp(log - top) for _, log in terms]
    total = weights[0]
    for weight in weights[1:]:
        total = total + weight
    columns = []
    for head in range(HEADS):
        at = slice(head * HD, (head + 1) * HD)
        row = None
        for (rows, _), weight in zip(terms, weights):
            term = weight[:, head : head + 1] * rows(at)
            row = term if row is None else row + term
        columns.append(row / total[:, head : head + 1])
    return columns, jnp.where(lane < HEADS, top + jnp.log(total), 0.0)


def packed_term(ref, index):
    rows = slice(index * ROWS, (index + 1) * ROWS)
    return (
        lambda at: ref[rows, at].astype(jnp.float32),
        join_parts(ref[rows, WIDE:].astype(jnp.float32)),
    )


def final_kernel(far_ref, own_ref, own_log_ref, out_ref):
    terms = [packed_term(far_ref, index) for index in range(ZH)]
    terms.append((lambda at: own_ref[:, at], own_log_ref[...]))
    columns, _ = merge(terms)
    for head in range(HEADS):
        out_ref[:, head * HD : (head + 1) * HD] = columns[head].astype(jnp.bfloat16)


def project_kernel(rows_ref, mine_ref, other_ref, out_ref, held, sems):
    pieces = 4
    length = GROUP * 64 // pieces
    copies = []
    for piece in range(pieces):
        source, first = (mine_ref, piece) if piece < pieces // 2 else (other_ref, piece - pieces // 2)
        copy = pltpu.make_async_copy(
            source.at[pl.ds(first * length, length), :], held.at[piece], sems.at[piece]
        )
        copy.start()
        copies.append(copy)
    for piece in range(pieces):
        copies[piece].wait()
        terms = lax.dot_general(
            held[piece], rows_ref[...], (((1,), (1,)), ((), ())), preferred_element_type=jnp.float32
        )
        for owner in range(length // 64):
            for part in range(XS):
                first = (owner * XS + part) * 16
                out_ref[part, piece * (length // 64) + owner] = terms[first : first + 16, :]


def sum_kernel(place_ref, terms_ref, out_ref):
    for far_core in range(CS):
        core = place_ref[2] if far_core == 0 else 1 - place_ref[2]
        for order, step in enumerate((0, 1, 3, 2)):
            y = lax.rem(place_ref[1] + step, YS)
            for far_side in range(ZP):
                side = place_ref[0] if far_side == 0 else 1 - place_ref[0]
                index = (far_core * YS + order) * ZP + far_side
                term = terms_ref[0, index]
                for part in range(1, XS):
                    term = term + terms_ref[part, index]
                out_ref[(side * YS + y) * CS + core] = term.astype(jnp.bfloat16)


def settle_kernel(place_ref, parts_ref, out_ref):
    place = place_ref[0]
    lane = lanes((16, 128))
    for side in range(ZP):
        parts = [
            parts_ref[side * YS * CS + owner].astype(jnp.float32) for owner in range(YS * CS)
        ]
        for half in range(ZQ):
            near = place if half == 0 else 1 - place
            for far in range(ZH):
                first = (half * ZH + far) * ROWS
                tile = jnp.zeros((16, 128), jnp.float32)
                for owner in range(YS * CS):
                    shift = (owner * ROWS - first) % 128
                    moved = parts[owner] if shift == 0 else pltpu.roll(parts[owner], shift, 1)
                    tile = jnp.where(lane // ROWS == owner, moved, tile)
                start = ((far * ZP + side) * ZQ + near) * 128
                out_ref[:, pl.ds(pl.multiple_of(start, 128), 128)] = tile.astype(jnp.bfloat16)


def own_partials(queries, own_keys, own_values, lengths):
    req_rows, q_heads, head_dim = queries.shape
    kv_heads = own_keys.shape[2]
    grouped = queries.reshape(req_rows, kv_heads, q_heads // kv_heads, head_dim)
    scores = jnp.einsum(
        "rhgd,rlhd->rhgl", grouped, own_keys, preferred_element_type=jnp.float32
    ) * head_dim ** (-0.5)
    visible = jnp.arange(own_keys.shape[1])[None, None, None, :] < lengths[:, None, None, None]
    scores = jnp.where(visible, scores, jnp.float32(-1e30))
    row_top = jnp.max(scores, axis=-1)
    exponent = jnp.exp(scores - row_top[..., None])
    row_total = jnp.sum(exponent, axis=-1)
    weights = exponent.astype(jnp.bfloat16)
    mixed_out = (
        jnp.einsum("rhgl,rlhd->rhgd", weights, own_values, preferred_element_type=jnp.float32)
        / row_total[..., None]
    )
    return (
        mixed_out.reshape(req_rows, q_heads * head_dim),
        (row_top + jnp.log(row_total)).reshape(req_rows, q_heads),
    )


def packed(rows):
    return jax.ShapeDtypeStruct((rows, PACK), jnp.bfloat16)


def inputs(near, far):
    return [pl.BlockSpec(memory_space=pltpu.VMEM)] * near + [
        pl.BlockSpec(memory_space=pltpu.HBM)
    ] * far


def spread_along(value, axis, count):
    copies = jnp.broadcast_to(value[None], (count,) + value.shape)
    everyone = lax.all_to_all(copies, axis, split_axis=0, concat_axis=0, tiled=True)
    return everyone.reshape((count * value.shape[0],) + value.shape[1:])


def on_device(
    queries,
    prefix_keys,
    prefix_values,
    suffix_keys,
    suffix_values,
    out_weight,
    prefix_lists,
    suffix_lengths,
    block_place,
):
    quad = ("zp", "zq", "y", "c")
    swap = [(0, 1), (1, 0)]
    flat_queries = queries.reshape(ROWS, WIDE)
    listed = jnp.pad(prefix_lists.astype(jnp.bfloat16), ((0, 0), (0, 120)))
    pool = spread_along(jnp.concatenate([flat_queries, listed], axis=1), "zh", ZH)

    up = [(place, (place + 1) % YS) for place in range(YS)]
    down = [(place, (place - 1) % YS) for place in range(YS)]
    turned = out_weight.T
    sides = jnp.concatenate([turned, lax.ppermute(turned, "zp", swap)], axis=0)
    above, below = lax.ppermute(sides, "y", down), lax.ppermute(sides, "y", up)
    across = [lax.ppermute(above[:64], "y", down), lax.ppermute(below[64:], "y", up)]
    mine = jnp.concatenate([sides, above, below] + across, axis=0)
    other = lax.ppermute(mine, "c", swap)

    lane = jnp.arange(128)
    stored = lax.axis_index("zh") * QUAD + lane
    here = (block_place[None, :] == stored[:, None]) & (lane < QUAD)[:, None]
    logical = jnp.sum(jnp.where(here, lane[None, :], 0), axis=1)
    logical = jnp.where(lane < QUAD, logical, -1).astype(jnp.float32)

    outgoing, select = pl.pallas_call(
        dispatch_kernel,
        in_specs=inputs(2, 1),
        out_shape=(
            jax.ShapeDtypeStruct((SLOTS, WIDE), jnp.bfloat16),
            jax.ShapeDtypeStruct((POOL, SLOTS), jnp.float32),
        ),
        compiler_params=PARAMS,
        name="dispatch",
    )(jnp.broadcast_to(logical[None], (8, 128)), pool, sides)
    arrived = lax.all_to_all(outgoing, quad, split_axis=0, concat_axis=0, tiled=True)
    partials = pl.pallas_call(
        attend_kernel,
        in_specs=inputs(3, 2),
        out_shape=packed(SLOTS),
        compiler_params=PARAMS,
        name="attend",
    )(
        arrived,
        prefix_keys.reshape(TOKENS, 2 * HD),
        prefix_values.reshape(TOKENS, 2 * HD),
        above,
        below,
    )
    back = lax.all_to_all(partials, quad, split_axis=0, concat_axis=0, tiled=True)
    joined = pl.pallas_call(
        gather_kernel,
        in_specs=inputs(2, 1),
        out_shape=packed(POOL),
        compiler_params=PARAMS,
        name="gather",
    )(back, select, mine)
    far = lax.all_to_all(joined, "zh", split_axis=0, concat_axis=0, tiled=True)

    own_out, own_log = own_partials(queries, suffix_keys, suffix_values, suffix_lengths)
    attended = pl.pallas_call(
        final_kernel,
        out_shape=jax.ShapeDtypeStruct((ROWS, WIDE), jnp.bfloat16),
        compiler_params=PARAMS,
        name="final",
    )(far, own_out, jnp.pad(own_log, ((0, 0), (0, 112))))

    rows = spread_along(attended, "zh", ZH)
    rows = jnp.concatenate([rows, lax.ppermute(rows, "zq", swap)], axis=0)
    terms = pl.pallas_call(
        project_kernel,
        in_specs=inputs(1, 2),
        out_shape=jax.ShapeDtypeStruct((XS, GROUP, 16, ZQ * POOL), jnp.float32),
        scratch_shapes=[
            pltpu.VMEM((4, GROUP * 64 // 4, WIDE), jnp.bfloat16),
            pltpu.SemaphoreType.DMA((4,)),
        ],
        compiler_params=PARAMS,
        name="project",
    )(rows, mine, other)
    terms = lax.all_to_all(terms, "kv", split_axis=0, concat_axis=0, tiled=True)
    one = [pl.BlockSpec(memory_space=pltpu.SMEM), pl.BlockSpec(memory_space=pltpu.VMEM)]
    place = jnp.stack([lax.axis_index(axis) for axis in ("zp", "y", "c")]).astype(jnp.int32)
    parts = pl.pallas_call(
        sum_kernel,
        in_specs=one,
        out_shape=jax.ShapeDtypeStruct((GROUP, 16, ZQ * POOL), jnp.bfloat16),
        compiler_params=PARAMS,
        name="sum",
    )(place, terms)
    parts = lax.all_to_all(parts, ("zp", "y", "c"), split_axis=0, concat_axis=0, tiled=True)
    return pl.pallas_call(
        settle_kernel,
        in_specs=one,
        out_shape=jax.ShapeDtypeStruct((16, ZH * QUAD * ROWS), jnp.bfloat16),
        compiler_params=PARAMS,
        name="settle",
    )(lax.axis_index("zq").reshape(1).astype(jnp.int32), parts).T


def solution(mesh):
    blk = ("zh", "zp", "zq", "y", "c")
    fine = Mesh(mesh.devices.reshape(ZH, ZP, ZQ, YS, CS, XS), blk + ("kv",))
    placed = (
        P(blk, "kv", None),
        P(blk, None, "kv", None),
        P(blk, None, "kv", None),
        P(blk, None, "kv", None),
        P(blk, None, "kv", None),
        P("kv", blk),
        P(blk, None),
        P(blk),
        P(),
    )
    return jax.shard_map(
        on_device, mesh=fine, in_specs=placed, out_specs=P(None, blk + ("kv",)), check_vma=False
    )
```

```python
import jax
import jax.numpy as jnp
from jax import lax
from jax.experimental import pallas as pl
from jax.experimental.pallas import tpu as pltpu
from jax.sharding import Mesh, PartitionSpec as P

ZH, ZP, ZQ, YS, CS, XS = 4, 2, 2, 4, 2, 4
QUAD = ZP * ZQ * YS * CS
GROUP = ZP * YS * CS
ROWS = 16
HEADS = 16
HD = 128
WIDE = HEADS * HD
PACK = WIDE + 128
POOL = ZH * ROWS
CAP = 2 * ZH
SLOTS = QUAD * CAP
TOKENS = 1024
FAR = -1e30
SCALE = HD ** -0.5
LOG2E = 1.4426950408889634
PARAMS = pltpu.CompilerParams(vmem_limit_bytes=40 * 1024 * 1024)


def lanes(shape):
    return lax.broadcasted_iota(jnp.int32, shape, len(shape) - 1)


def split_parts(value):
    high = value.astype(jnp.bfloat16).astype(jnp.float32)
    rest = value - high
    middle = rest.astype(jnp.bfloat16).astype(jnp.float32)
    low = (rest - middle).astype(jnp.bfloat16).astype(jnp.float32)
    return high + pltpu.roll(middle, 16, 1) + pltpu.roll(low, 32, 1)


def join_parts(packed):
    whole = packed + pltpu.roll(packed, 112, 1) + pltpu.roll(packed, 96, 1)
    return jnp.where(lanes(whole.shape) < HEADS, whole, 0.0)


def dispatch_kernel(logical_ref, pool_ref, above_ref, below_ref, out_ref, select_ref):
    listed = pool_ref[:, WIDE:].astype(jnp.float32)
    logical = logical_ref[0:1, :]
    hot = jnp.zeros((POOL, 128), jnp.float32)
    for item in range(8):
        hot = jnp.where(listed[:, item : item + 1] == logical, 1.0, hot)
    hot = hot.astype(jnp.bfloat16)
    row = lax.broadcasted_iota(jnp.int32, (POOL, POOL), 0)
    column = lax.broadcasted_iota(jnp.int32, (POOL, POOL), 1)
    earlier = jnp.where(row > column, 1.0, 0.0).astype(jnp.bfloat16)
    rank = jnp.dot(earlier, hot, preferred_element_type=jnp.float32).astype(jnp.bfloat16)
    owner = lax.broadcasted_iota(jnp.int32, (128, SLOTS), 0)
    slot = lax.broadcasted_iota(jnp.int32, (128, SLOTS), 1)
    spread = jnp.where(slot // CAP == owner, 1.0, 0.0).astype(jnp.bfloat16)
    hot_at = jnp.dot(hot, spread, preferred_element_type=jnp.float32)
    rank_at = jnp.dot(rank, spread, preferred_element_type=jnp.float32)
    wanted = (lanes((POOL, SLOTS)) % CAP).astype(jnp.float32)
    select = jnp.where((hot_at > 0.5) & (rank_at == wanted), 1.0, 0.0)
    select_ref[...] = select
    out_ref[...] = lax.dot_general(
        select.astype(jnp.bfloat16),
        pool_ref[:, :WIDE],
        (((0,), (0,)), ((), ())),
        preferred_element_type=jnp.float32,
    ).astype(jnp.bfloat16)


def attend_kernel(q_ref, k_ref, v_ref, weight_ref, facing_ref, own_ref, out_ref):
    logs = jnp.zeros((SLOTS, 128), jnp.float32)
    lane = lanes((SLOTS, 128))

    def scores_of(head):
        group = slice((head // 8) * HD, (head // 8 + 1) * HD)
        return lax.dot_general(
            q_ref[:, head * HD : (head + 1) * HD],
            k_ref[:, group],
            (((1,), (1,)), ((), ())),
            preferred_element_type=jnp.float32,
        )

    coming = scores_of(0)
    for head in range(HEADS):
        scores = coming
        if head + 1 < HEADS:
            coming = scores_of(head + 1)
        group = slice((head // 8) * HD, (head // 8 + 1) * HD)
        at = slice(head * HD, (head + 1) * HD)
        top = jnp.max(scores, axis=1, keepdims=True)
        grown = jnp.exp2((scores - top) * (SCALE * LOG2E))
        total = jnp.sum(grown, axis=1, keepdims=True)
        mixed = jnp.dot(
            grown.astype(jnp.bfloat16), v_ref[:, group], preferred_element_type=jnp.float32
        )
        out_ref[:, at] = (mixed / total).astype(jnp.bfloat16)
        logs = jnp.where(lane == head, top * SCALE + jnp.log(total), logs)
    out_ref[:, WIDE:] = split_parts(logs).astype(jnp.bfloat16)


def gather_kernel(back_ref, select_ref, weight_ref, facing_ref, joined_ref):
    chosen = select_ref[...] > 0.5
    slot_logs = join_parts(back_ref[:, WIDE:].astype(jnp.float32)).T
    lane = lanes((POOL, 128))
    logs = jnp.zeros((POOL, 128), jnp.float32)
    for head in range(HEADS):
        at = slice(head * HD, (head + 1) * HD)
        log = jnp.where(chosen, slot_logs[head : head + 1, :], FAR)
        top = jnp.max(log, axis=1, keepdims=True)
        grown = jnp.where(chosen, jnp.exp(log - top), 0.0)
        total = jnp.maximum(jnp.sum(grown, axis=1, keepdims=True), 0.5)
        weight = grown / total
        high = weight.astype(jnp.bfloat16)
        low = (weight - high.astype(jnp.float32)).astype(jnp.bfloat16)
        mixed = jnp.dot(high, back_ref[:, at], preferred_element_type=jnp.float32)
        mixed = mixed + jnp.dot(low, back_ref[:, at], preferred_element_type=jnp.float32)
        joined_ref[:, at] = mixed.astype(jnp.bfloat16)
        logs = jnp.where(lane == head, top + jnp.log(total), logs)
    joined_ref[:, WIDE:] = split_parts(logs).astype(jnp.bfloat16)


def merge(terms):
    top = terms[0][1]
    for _, log in terms[1:]:
        top = jnp.maximum(top, log)
    lane = lanes((ROWS, 128))
    weights = [jnp.exp(log - top) for _, log in terms]
    total = weights[0]
    for weight in weights[1:]:
        total = total + weight
    columns = []
    for head in range(HEADS):
        at = slice(head * HD, (head + 1) * HD)
        row = None
        for (rows, _), weight in zip(terms, weights):
            term = weight[:, head : head + 1] * rows(at)
            row = term if row is None else row + term
        columns.append(row / total[:, head : head + 1])
    return columns, jnp.where(lane < HEADS, top + jnp.log(total), 0.0)


def packed_term(ref, index):
    rows = slice(index * ROWS, (index + 1) * ROWS)
    return (
        lambda at: ref[rows, at].astype(jnp.float32),
        join_parts(ref[rows, WIDE:].astype(jnp.float32)),
    )


def final_kernel(far_ref, own_ref, own_log_ref, weight_ref, out_ref):
    terms = [packed_term(far_ref, index) for index in range(ZH)]
    terms.append((lambda at: own_ref[:, at], own_log_ref[...]))
    columns, _ = merge(terms)
    for head in range(HEADS):
        out_ref[:, head * HD : (head + 1) * HD] = columns[head].astype(jnp.bfloat16)


def project_kernel(rows_ref, *refs):
    sources, out_ref, held, sems = refs[:4], refs[4], refs[5], refs[6]
    copies = []
    for piece, source in enumerate(sources):
        copy = pltpu.make_async_copy(source, held.at[piece], sems.at[piece])
        copy.start()
        copies.append(copy)
    for piece in range(4):
        copies[piece].wait()
        terms = lax.dot_general(
            held[piece], rows_ref[...], (((1,), (1,)), ((), ())), preferred_element_type=jnp.float32
        )
        for owner in range(YS):
            for part in range(XS):
                first = (owner * XS + part) * 16
                out_ref[part, piece * YS + owner] = terms[first : first + 16, :]


def sum_kernel(place_ref, terms_ref, out_ref):
    for far_side in range(ZP):
        side = place_ref[0] if far_side == 0 else 1 - place_ref[0]
        for far_core in range(CS):
            core = place_ref[2] if far_core == 0 else 1 - place_ref[2]
            for order, step in enumerate((0, 1, 3, 2)):
                y = lax.rem(place_ref[1] + step, YS)
                index = (far_side * CS + far_core) * YS + order
                term = terms_ref[0, index]
                for part in range(1, XS):
                    term = term + terms_ref[part, index]
                out_ref[(side * YS + y) * CS + core] = term.astype(jnp.bfloat16)


def settle_kernel(place_ref, parts_ref, out_ref):
    place = place_ref[0]
    lane = lanes((16, 128))
    for side in range(ZP):
        parts = [
            parts_ref[side * YS * CS + owner].astype(jnp.float32) for owner in range(YS * CS)
        ]
        for half in range(ZQ):
            near = place if half == 0 else 1 - place
            for far in range(ZH):
                first = (half * ZH + far) * ROWS
                tile = jnp.zeros((16, 128), jnp.float32)
                for owner in range(YS * CS):
                    shift = (owner * ROWS - first) % 128
                    moved = parts[owner] if shift == 0 else pltpu.roll(parts[owner], shift, 1)
                    tile = jnp.where(lane // ROWS == owner, moved, tile)
                start = ((far * ZP + side) * ZQ + near) * 128
                out_ref[:, pl.ds(pl.multiple_of(start, 128), 128)] = tile.astype(jnp.bfloat16)


def own_partials(queries, own_keys, own_values, lengths):
    req_rows, q_heads, head_dim = queries.shape
    kv_heads = own_keys.shape[2]
    grouped = queries.reshape(req_rows, kv_heads, q_heads // kv_heads, head_dim)
    scores = jnp.einsum(
        "rhgd,rlhd->rhgl", grouped, own_keys, preferred_element_type=jnp.float32
    ) * head_dim ** (-0.5)
    visible = jnp.arange(own_keys.shape[1])[None, None, None, :] < lengths[:, None, None, None]
    scores = jnp.where(visible, scores, jnp.float32(-1e30))
    row_top = jnp.max(scores, axis=-1)
    exponent = jnp.exp(scores - row_top[..., None])
    row_total = jnp.sum(exponent, axis=-1)
    weights = exponent.astype(jnp.bfloat16)
    mixed_out = (
        jnp.einsum("rhgl,rlhd->rhgd", weights, own_values, preferred_element_type=jnp.float32)
        / row_total[..., None]
    )
    return (
        mixed_out.reshape(req_rows, q_heads * head_dim),
        (row_top + jnp.log(row_total)).reshape(req_rows, q_heads),
    )


def packed(rows):
    return jax.ShapeDtypeStruct((rows, PACK), jnp.bfloat16)


def inputs(near, far):
    return [pl.BlockSpec(memory_space=pltpu.VMEM)] * near + [
        pl.BlockSpec(memory_space=pltpu.HBM)
    ] * far


def spread_along(value, axis, count):
    copies = jnp.broadcast_to(value[None], (count,) + value.shape)
    everyone = lax.all_to_all(copies, axis, split_axis=0, concat_axis=0, tiled=True)
    return everyone.reshape((count * value.shape[0],) + value.shape[1:])


def on_device(
    queries,
    prefix_keys,
    prefix_values,
    suffix_keys,
    suffix_values,
    out_weight,
    prefix_lists,
    suffix_lengths,
    block_place,
):
    quad = ("zp", "zq", "y", "c")
    swap = [(0, 1), (1, 0)]
    flat_queries = queries.reshape(ROWS, WIDE)
    listed = jnp.pad(prefix_lists.astype(jnp.bfloat16), ((0, 0), (0, 120)))
    pool = spread_along(jnp.concatenate([flat_queries, listed], axis=1), "zh", ZH)

    up = [(place, (place + 1) % YS) for place in range(YS)]
    down = [(place, (place - 1) % YS) for place in range(YS)]

    def beside(block):
        return lax.ppermute(block, "y", down), lax.ppermute(block, "y", up)

    def piece_of(block, above, below):
        across = [lax.ppermute(above[:32], "y", down), lax.ppermute(below[32:], "y", up)]
        return jnp.concatenate([block, above, below] + across, axis=0)

    turned = out_weight.T
    facing = lax.ppermute(turned, "zp", swap)
    above, below = beside(turned)
    mine = piece_of(turned, above, below)
    mine_far = piece_of(facing, *beside(facing))
    other = lax.ppermute(mine, "c", swap)
    other_far = lax.ppermute(mine_far, "c", swap)
    own_out, own_log = own_partials(queries, suffix_keys, suffix_values, suffix_lengths)

    lane = jnp.arange(128)
    stored = lax.axis_index("zh") * QUAD + lane
    here = (block_place[None, :] == stored[:, None]) & (lane < QUAD)[:, None]
    logical = jnp.sum(jnp.where(here, lane[None, :], 0), axis=1)
    logical = jnp.where(lane < QUAD, logical, -1).astype(jnp.float32)

    outgoing, select = pl.pallas_call(
        dispatch_kernel,
        in_specs=inputs(2, 2),
        out_shape=(
            jax.ShapeDtypeStruct((SLOTS, WIDE), jnp.bfloat16),
            jax.ShapeDtypeStruct((POOL, SLOTS), jnp.float32),
        ),
        compiler_params=PARAMS,
        name="dispatch",
    )(jnp.broadcast_to(logical[None], (8, 128)), pool, above, below)
    arrived = lax.all_to_all(outgoing, quad, split_axis=0, concat_axis=0, tiled=True)
    partials = pl.pallas_call(
        attend_kernel,
        in_specs=inputs(3, 3),
        out_shape=packed(SLOTS),
        compiler_params=PARAMS,
        name="attend",
    )(
        arrived,
        prefix_keys.reshape(TOKENS, 2 * HD),
        prefix_values.reshape(TOKENS, 2 * HD),
        mine,
        facing,
        own_out,
    )
    back = lax.all_to_all(partials, quad, split_axis=0, concat_axis=0, tiled=True)
    joined = pl.pallas_call(
        gather_kernel,
        in_specs=inputs(2, 2),
        out_shape=packed(POOL),
        compiler_params=PARAMS,
        name="gather",
    )(back, select, other, mine_far)
    far = lax.all_to_all(joined, "zh", split_axis=0, concat_axis=0, tiled=True)

    attended = pl.pallas_call(
        final_kernel,
        in_specs=inputs(3, 1),
        out_shape=jax.ShapeDtypeStruct((ROWS, WIDE), jnp.bfloat16),
        compiler_params=PARAMS,
        name="final",
    )(far, own_out, jnp.pad(own_log, ((0, 0), (0, 112))), other_far)

    rows = spread_along(attended, "zh", ZH)
    rows = jnp.concatenate([rows, lax.ppermute(rows, "zq", swap)], axis=0)
    terms = pl.pallas_call(
        project_kernel,
        in_specs=inputs(1, 4),
        out_shape=jax.ShapeDtypeStruct((XS, GROUP, 16, ZQ * POOL), jnp.float32),
        scratch_shapes=[
            pltpu.VMEM((4, GROUP * 64 // 4, WIDE), jnp.bfloat16),
            pltpu.SemaphoreType.DMA((4,)),
        ],
        compiler_params=PARAMS,
        name="project",
    )(rows, mine, other, mine_far, other_far)
    terms = lax.all_to_all(terms, "kv", split_axis=0, concat_axis=0, tiled=True)
    one = [pl.BlockSpec(memory_space=pltpu.SMEM), pl.BlockSpec(memory_space=pltpu.VMEM)]
    place = jnp.stack([lax.axis_index(axis) for axis in ("zp", "y", "c")]).astype(jnp.int32)
    parts = pl.pallas_call(
        sum_kernel,
        in_specs=one,
        out_shape=jax.ShapeDtypeStruct((GROUP, 16, ZQ * POOL), jnp.bfloat16),
        compiler_params=PARAMS,
        name="sum",
    )(place, terms)
    parts = lax.all_to_all(parts, ("zp", "y", "c"), split_axis=0, concat_axis=0, tiled=True)
    return pl.pallas_call(
        settle_kernel,
        in_specs=one,
        out_shape=jax.ShapeDtypeStruct((16, ZH * QUAD * ROWS), jnp.bfloat16),
        compiler_params=PARAMS,
        name="settle",
    )(lax.axis_index("zq").reshape(1).astype(jnp.int32), parts).T


def solution(mesh):
    blk = ("zh", "zp", "zq", "y", "c")
    fine = Mesh(mesh.devices.reshape(ZH, ZP, ZQ, YS, CS, XS), blk + ("kv",))
    placed = (
        P(blk, "kv", None),
        P(blk, None, "kv", None),
        P(blk, None, "kv", None),
        P(blk, None, "kv", None),
        P(blk, None, "kv", None),
        P("kv", blk),
        P(blk, None),
        P(blk),
        P(),
    )
    return jax.shard_map(
        on_device, mesh=fine, in_specs=placed, out_specs=P(None, blk + ("kv",)), check_vma=False
    )
```

```python
import jax
import jax.numpy as jnp
from jax import lax
from jax.experimental import pallas as pl
from jax.experimental.pallas import tpu as pltpu
from jax.sharding import Mesh, PartitionSpec as P

ZH, ZP, ZQ, YS, CS, XS = 4, 2, 2, 4, 2, 4
QUAD = ZP * ZQ * YS * CS
GROUP = ZQ * YS * CS
ROWS = 16
HEADS = 16
HD = 128
WIDE = HEADS * HD
PACK = WIDE + 128
POOL = ZH * ROWS
CAP = 2 * ZH
SLOTS = QUAD * CAP
TOKENS = 1024
FAR = -1e30
SCALE = HD ** -0.5
LOG2E = 1.4426950408889634
PARAMS = pltpu.CompilerParams(vmem_limit_bytes=20 * 1024 * 1024)


def lanes(shape):
    return lax.broadcasted_iota(jnp.int32, shape, len(shape) - 1)


def split_parts(value):
    high = value.astype(jnp.bfloat16).astype(jnp.float32)
    rest = value - high
    middle = rest.astype(jnp.bfloat16).astype(jnp.float32)
    low = (rest - middle).astype(jnp.bfloat16).astype(jnp.float32)
    return high + pltpu.roll(middle, 16, 1) + pltpu.roll(low, 32, 1)


def join_parts(packed):
    whole = packed + pltpu.roll(packed, 112, 1) + pltpu.roll(packed, 96, 1)
    return jnp.where(lanes(whole.shape) < HEADS, whole, 0.0)


def dispatch_kernel(logical_ref, pool_ref, above_ref, below_ref, out_ref, select_ref):
    listed = pool_ref[:, WIDE:].astype(jnp.float32)
    logical = logical_ref[0:1, :]
    hot = jnp.zeros((POOL, 128), jnp.float32)
    for item in range(8):
        hot = jnp.where(listed[:, item : item + 1] == logical, 1.0, hot)
    hot = hot.astype(jnp.bfloat16)
    row = lax.broadcasted_iota(jnp.int32, (POOL, POOL), 0)
    column = lax.broadcasted_iota(jnp.int32, (POOL, POOL), 1)
    earlier = jnp.where(row > column, 1.0, 0.0).astype(jnp.bfloat16)
    rank = jnp.dot(earlier, hot, preferred_element_type=jnp.float32).astype(jnp.bfloat16)
    owner = lax.broadcasted_iota(jnp.int32, (128, SLOTS), 0)
    slot = lax.broadcasted_iota(jnp.int32, (128, SLOTS), 1)
    spread = jnp.where(slot // CAP == owner, 1.0, 0.0).astype(jnp.bfloat16)
    hot_at = jnp.dot(hot, spread, preferred_element_type=jnp.float32)
    rank_at = jnp.dot(rank, spread, preferred_element_type=jnp.float32)
    wanted = (lanes((POOL, SLOTS)) % CAP).astype(jnp.float32)
    select = jnp.where((hot_at > 0.5) & (rank_at == wanted), 1.0, 0.0)
    select_ref[...] = select
    out_ref[...] = lax.dot_general(
        select.astype(jnp.bfloat16),
        pool_ref[:, :WIDE],
        (((0,), (0,)), ((), ())),
        preferred_element_type=jnp.float32,
    ).astype(jnp.bfloat16)


def attend_kernel(q_ref, k_ref, v_ref, weight_ref, facing_ref, own_ref, out_ref):
    logs = jnp.zeros((SLOTS, 128), jnp.float32)
    lane = lanes((SLOTS, 128))

    def scores_of(head):
        group = slice((head // 8) * HD, (head // 8 + 1) * HD)
        return lax.dot_general(
            q_ref[:, head * HD : (head + 1) * HD],
            k_ref[:, group],
            (((1,), (1,)), ((), ())),
            preferred_element_type=jnp.float32,
        )

    coming = scores_of(0)
    for head in range(HEADS):
        scores = coming
        if head + 1 < HEADS:
            coming = scores_of(head + 1)
        group = slice((head // 8) * HD, (head // 8 + 1) * HD)
        at = slice(head * HD, (head + 1) * HD)
        top = jnp.max(scores, axis=1, keepdims=True)
        grown = jnp.exp2((scores - top) * (SCALE * LOG2E))
        total = jnp.sum(grown, axis=1, keepdims=True)
        mixed = jnp.dot(
            grown.astype(jnp.bfloat16), v_ref[:, group], preferred_element_type=jnp.float32
        )
        out_ref[:, at] = (mixed / total).astype(jnp.bfloat16)
        logs = jnp.where(lane == head, top * SCALE + jnp.log(total), logs)
    out_ref[:, WIDE:] = split_parts(logs).astype(jnp.bfloat16)


def gather_kernel(back_ref, select_ref, weight_ref, above_ref, below_ref, joined_ref):
    chosen = select_ref[...] > 0.5
    slot_logs = join_parts(back_ref[:, WIDE:].astype(jnp.float32)).T
    lane = lanes((POOL, 128))
    logs = jnp.zeros((POOL, 128), jnp.float32)
    for head in range(HEADS):
        at = slice(head * HD, (head + 1) * HD)
        log = jnp.where(chosen, slot_logs[head : head + 1, :], FAR)
        top = jnp.max(log, axis=1, keepdims=True)
        grown = jnp.where(chosen, jnp.exp(log - top), 0.0)
        total = jnp.maximum(jnp.sum(grown, axis=1, keepdims=True), 0.5)
        weight = grown / total
        high = weight.astype(jnp.bfloat16)
        low = (weight - high.astype(jnp.float32)).astype(jnp.bfloat16)
        mixed = jnp.dot(high, back_ref[:, at], preferred_element_type=jnp.float32)
        mixed = mixed + jnp.dot(low, back_ref[:, at], preferred_element_type=jnp.float32)
        joined_ref[:, at] = mixed.astype(jnp.bfloat16)
        logs = jnp.where(lane == head, top + jnp.log(total), logs)
    joined_ref[:, WIDE:] = split_parts(logs).astype(jnp.bfloat16)


def merge(terms):
    top = terms[0][1]
    for _, log in terms[1:]:
        top = jnp.maximum(top, log)
    lane = lanes((ROWS, 128))
    weights = [jnp.exp(log - top) for _, log in terms]
    total = weights[0]
    for weight in weights[1:]:
        total = total + weight
    columns = []
    for head in range(HEADS):
        at = slice(head * HD, (head + 1) * HD)
        row = None
        for (rows, _), weight in zip(terms, weights):
            term = weight[:, head : head + 1] * rows(at)
            row = term if row is None else row + term
        columns.append(row / total[:, head : head + 1])
    return columns, jnp.where(lane < HEADS, top + jnp.log(total), 0.0)


def packed_term(ref, index):
    rows = slice(index * ROWS, (index + 1) * ROWS)
    return (
        lambda at: ref[rows, at].astype(jnp.float32),
        join_parts(ref[rows, WIDE:].astype(jnp.float32)),
    )


def final_kernel(far_ref, own_ref, own_log_ref, weight_ref, out_ref):
    terms = [packed_term(far_ref, index) for index in range(ZH)]
    terms.append((lambda at: own_ref[:, at], own_log_ref[...]))
    columns, _ = merge(terms)
    for head in range(HEADS):
        out_ref[:, head * HD : (head + 1) * HD] = columns[head].astype(jnp.bfloat16)


def project_kernel(rows_ref, *refs):
    sources, out_ref, held, sems = refs[:4], refs[4], refs[5], refs[6]
    copies = []
    for piece, source in enumerate(sources):
        copy = pltpu.make_async_copy(source, held.at[piece], sems.at[piece])
        copy.start()
        copies.append(copy)
    for piece in range(4):
        copies[piece].wait()
        terms = lax.dot_general(
            held[piece], rows_ref[...], (((1,), (1,)), ((), ())), preferred_element_type=jnp.float32
        )
        for owner in range(YS):
            for part in range(XS):
                first = (owner * XS + part) * 16
                out_ref[part, piece * YS + owner] = terms[first : first + 16, :]


def sum_kernel(place_ref, terms_ref, out_ref):
    for far_side in range(ZQ):
        side = place_ref[0] if far_side == 0 else 1 - place_ref[0]
        for far_core in range(CS):
            core = place_ref[2] if far_core == 0 else 1 - place_ref[2]
            for order, step in enumerate((0, 1, 3, 2)):
                y = lax.rem(place_ref[1] + step, YS)
                index = (far_side * CS + far_core) * YS + order
                term = terms_ref[0, index]
                for part in range(1, XS):
                    term = term + terms_ref[part, index]
                out_ref[(side * YS + y) * CS + core] = term.astype(jnp.bfloat16)


def settle_kernel(parts_ref, out_ref):
    lane = lanes((16, 128))
    for side in range(ZQ):
        parts = [
            parts_ref[side * YS * CS + owner].astype(jnp.float32) for owner in range(YS * CS)
        ]
        for far in range(ZH * ZP):
            tile = jnp.zeros((16, 128), jnp.float32)
            for owner in range(YS * CS):
                shift = (owner - far) * ROWS % 128
                moved = parts[owner] if shift == 0 else pltpu.roll(parts[owner], shift, 1)
                tile = jnp.where(lane // ROWS == owner, moved, tile)
            start = (far * ZQ + side) * 128
            out_ref[:, start : start + 128] = tile.astype(jnp.bfloat16)


def own_partials(queries, own_keys, own_values, lengths):
    req_rows, q_heads, head_dim = queries.shape
    kv_heads = own_keys.shape[2]
    grouped = queries.reshape(req_rows, kv_heads, q_heads // kv_heads, head_dim)
    scores = jnp.einsum(
        "rhgd,rlhd->rhgl", grouped, own_keys, preferred_element_type=jnp.float32
    ) * head_dim ** (-0.5)
    visible = jnp.arange(own_keys.shape[1])[None, None, None, :] < lengths[:, None, None, None]
    scores = jnp.where(visible, scores, jnp.float32(-1e30))
    row_top = jnp.max(scores, axis=-1)
    exponent = jnp.exp(scores - row_top[..., None])
    row_total = jnp.sum(exponent, axis=-1)
    weights = exponent.astype(jnp.bfloat16)
    mixed_out = (
        jnp.einsum("rhgl,rlhd->rhgd", weights, own_values, preferred_element_type=jnp.float32)
        / row_total[..., None]
    )
    return (
        mixed_out.reshape(req_rows, q_heads * head_dim),
        (row_top + jnp.log(row_total)).reshape(req_rows, q_heads),
    )


def packed(rows):
    return jax.ShapeDtypeStruct((rows, PACK), jnp.bfloat16)


def inputs(near, far):
    return [pl.BlockSpec(memory_space=pltpu.VMEM)] * near + [
        pl.BlockSpec(memory_space=pl.ANY)
    ] * far


def spread_along(value, axis, count):
    copies = jnp.broadcast_to(value[None], (count,) + value.shape)
    everyone = lax.all_to_all(copies, axis, split_axis=0, concat_axis=0, tiled=True)
    return everyone.reshape((count * value.shape[0],) + value.shape[1:])


def on_device(
    queries,
    prefix_keys,
    prefix_values,
    suffix_keys,
    suffix_values,
    out_weight,
    prefix_lists,
    suffix_lengths,
    block_place,
):
    quad = ("zp", "zq", "y", "c")
    swap = [(0, 1), (1, 0)]
    flat_queries = queries.reshape(ROWS, WIDE)
    listed = jnp.pad(prefix_lists.astype(jnp.bfloat16), ((0, 0), (0, 120)))
    pool = spread_along(jnp.concatenate([flat_queries, listed], axis=1), "zh", ZH)

    up = [(place, (place + 1) % YS) for place in range(YS)]
    down = [(place, (place - 1) % YS) for place in range(YS)]

    def beside(block):
        return lax.ppermute(block, "y", down), lax.ppermute(block, "y", up)

    def piece_of(block, above, below):
        across = [lax.ppermute(above[:32], "y", down), lax.ppermute(below[32:], "y", up)]
        return jnp.concatenate([block, above, below] + across, axis=0)

    turned = out_weight.T
    facing = lax.ppermute(turned, "zq", swap)
    above, below = beside(turned)
    mine = piece_of(turned, above, below)
    above_far, below_far = beside(facing)
    mine_far = piece_of(facing, above_far, below_far)
    other = lax.ppermute(mine, "c", swap)
    other_far = lax.ppermute(mine_far, "c", swap)
    own_out, own_log = own_partials(queries, suffix_keys, suffix_values, suffix_lengths)

    lane = jnp.arange(128)
    stored = lax.axis_index("zh") * QUAD + lane
    here = (block_place[None, :] == stored[:, None]) & (lane < QUAD)[:, None]
    logical = jnp.sum(jnp.where(here, lane[None, :], 0), axis=1)
    logical = jnp.where(lane < QUAD, logical, -1).astype(jnp.float32)

    outgoing, select = pl.pallas_call(
        dispatch_kernel,
        in_specs=inputs(2, 2),
        out_shape=(
            jax.ShapeDtypeStruct((SLOTS, WIDE), jnp.bfloat16),
            jax.ShapeDtypeStruct((POOL, SLOTS), jnp.float32),
        ),
        compiler_params=PARAMS,
        name="dispatch",
    )(jnp.broadcast_to(logical[None], (8, 128)), pool, above, below)
    arrived = lax.all_to_all(outgoing, quad, split_axis=0, concat_axis=0, tiled=True)
    partials = pl.pallas_call(
        attend_kernel,
        in_specs=inputs(3, 3),
        out_shape=packed(SLOTS),
        compiler_params=PARAMS,
        name="attend",
    )(
        arrived,
        prefix_keys.reshape(TOKENS, 2 * HD),
        prefix_values.reshape(TOKENS, 2 * HD),
        mine,
        facing,
        own_out,
    )
    back = lax.all_to_all(partials, quad, split_axis=0, concat_axis=0, tiled=True)
    joined = pl.pallas_call(
        gather_kernel,
        in_specs=inputs(2, 3),
        out_shape=packed(POOL),
        compiler_params=PARAMS,
        name="gather",
    )(back, select, other, above_far, below_far)
    far = lax.all_to_all(joined, "zh", split_axis=0, concat_axis=0, tiled=True)

    attended = pl.pallas_call(
        final_kernel,
        in_specs=inputs(3, 1),
        out_shape=jax.ShapeDtypeStruct((ROWS, WIDE), jnp.bfloat16),
        compiler_params=PARAMS,
        name="final",
    )(far, own_out, jnp.pad(own_log, ((0, 0), (0, 112))), mine_far)

    rows = spread_along(attended, ("zh", "zp"), ZH * ZP)
    terms = pl.pallas_call(
        project_kernel,
        in_specs=inputs(1, 4),
        out_shape=jax.ShapeDtypeStruct((XS, GROUP, 16, ZP * POOL), jnp.float32),
        scratch_shapes=[
            pltpu.VMEM((4, YS * 64, WIDE), jnp.bfloat16),
            pltpu.SemaphoreType.DMA((4,)),
        ],
        compiler_params=PARAMS,
        name="project",
    )(rows, mine, other, mine_far, other_far)
    terms = lax.all_to_all(terms, "kv", split_axis=0, concat_axis=0, tiled=True)
    place = jnp.stack([lax.axis_index(axis) for axis in ("zq", "y", "c")]).astype(jnp.int32)
    parts = pl.pallas_call(
        sum_kernel,
        in_specs=[
            pl.BlockSpec(memory_space=pltpu.SMEM),
            pl.BlockSpec(memory_space=pltpu.VMEM),
        ],
        out_shape=jax.ShapeDtypeStruct((GROUP, 16, ZP * POOL), jnp.bfloat16),
        compiler_params=PARAMS,
        name="sum",
    )(place, terms)
    parts = lax.all_to_all(parts, ("zq", "y", "c"), split_axis=0, concat_axis=0, tiled=True)
    return pl.pallas_call(
        settle_kernel,
        out_shape=jax.ShapeDtypeStruct((16, ZH * QUAD * ROWS), jnp.bfloat16),
        compiler_params=PARAMS,
        name="settle",
    )(parts).T


def solution(mesh):
    blk = ("zh", "zp", "zq", "y", "c")
    fine = Mesh(mesh.devices.reshape(ZH, ZP, ZQ, YS, CS, XS), blk + ("kv",))
    placed = (
        P(blk, "kv", None),
        P(blk, None, "kv", None),
        P(blk, None, "kv", None),
        P(blk, None, "kv", None),
        P(blk, None, "kv", None),
        P("kv", blk),
        P(blk, None),
        P(blk),
        P(),
    )
    return jax.shard_map(
        on_device, mesh=fine, in_specs=placed, out_specs=P(None, blk + ("kv",)), check_vma=False
    )
```

```python
import jax
import jax.numpy as jnp
from jax import lax
from jax.experimental import pallas as pl
from jax.experimental.pallas import tpu as pltpu
from jax.sharding import Mesh, PartitionSpec as P

ZH, ZP, ZQ, YS, CS, XS = 4, 2, 2, 4, 2, 4
QUAD = ZP * ZQ * YS * CS
GROUP = ZQ * YS * CS
ROWS = 16
HEADS = 16
HD = 128
WIDE = HEADS * HD
PACK = WIDE + 128
POOL = ZH * ROWS
CAP = 2 * ZH
SLOTS = QUAD * CAP
TOKENS = 1024
FAR = -1e30
SCALE = HD ** -0.5
LOG2E = 1.4426950408889634
PARAMS = pltpu.CompilerParams(vmem_limit_bytes=20 * 1024 * 1024)


def lanes(shape):
    return lax.broadcasted_iota(jnp.int32, shape, len(shape) - 1)


def split_parts(value):
    high = value.astype(jnp.bfloat16).astype(jnp.float32)
    rest = value - high
    middle = rest.astype(jnp.bfloat16).astype(jnp.float32)
    low = (rest - middle).astype(jnp.bfloat16).astype(jnp.float32)
    return high + pltpu.roll(middle, 16, 1) + pltpu.roll(low, 32, 1)


def join_parts(packed):
    whole = packed + pltpu.roll(packed, 112, 1) + pltpu.roll(packed, 96, 1)
    return jnp.where(lanes(whole.shape) < HEADS, whole, 0.0)


def prepare_kernel(queries_ref, listed_ref, out_ref):
    place = lax.broadcasted_iota(jnp.int32, (8, 128), 0)
    spread = jnp.where(lanes((8, 128)) == place, 1.0, 0.0).astype(jnp.bfloat16)
    listed = lax.dot_general(
        listed_ref[...].astype(jnp.float32).astype(jnp.bfloat16),
        spread,
        (((0,), (0,)), ((), ())),
        preferred_element_type=jnp.float32,
    ).astype(jnp.bfloat16)
    heads = [queries_ref[:, head, :] for head in range(HEADS)]
    for copy in range(ZH):
        for head in range(HEADS):
            out_ref[copy, :, head * HD : (head + 1) * HD] = heads[head]
        out_ref[copy, :, WIDE:] = listed


def dispatch_kernel(logical_ref, pool_ref, above_ref, below_ref, out_ref, select_ref):
    listed = pool_ref[:, WIDE:].astype(jnp.float32)
    logical = logical_ref[0:1, :]
    hot = jnp.zeros((POOL, 128), jnp.float32)
    for item in range(8):
        hot = jnp.where(listed[:, item : item + 1] == logical, 1.0, hot)
    hot = hot.astype(jnp.bfloat16)
    row = lax.broadcasted_iota(jnp.int32, (POOL, POOL), 0)
    column = lax.broadcasted_iota(jnp.int32, (POOL, POOL), 1)
    earlier = jnp.where(row > column, 1.0, 0.0).astype(jnp.bfloat16)
    rank = jnp.dot(earlier, hot, preferred_element_type=jnp.float32).astype(jnp.bfloat16)
    owner = lax.broadcasted_iota(jnp.int32, (128, SLOTS), 0)
    slot = lax.broadcasted_iota(jnp.int32, (128, SLOTS), 1)
    spread = jnp.where(slot // CAP == owner, 1.0, 0.0).astype(jnp.bfloat16)
    hot_at = jnp.dot(hot, spread, preferred_element_type=jnp.float32)
    rank_at = jnp.dot(rank, spread, preferred_element_type=jnp.float32)
    wanted = (lanes((POOL, SLOTS)) % CAP).astype(jnp.float32)
    select = jnp.where((hot_at > 0.5) & (rank_at == wanted), 1.0, 0.0)
    select_ref[...] = select
    out_ref[...] = lax.dot_general(
        select.astype(jnp.bfloat16),
        pool_ref[:, :WIDE],
        (((0,), (0,)), ((), ())),
        preferred_element_type=jnp.float32,
    ).astype(jnp.bfloat16)


def attend_kernel(q_ref, k_ref, v_ref, weight_ref, facing_ref, own_ref, out_ref):
    logs = jnp.zeros((SLOTS, 128), jnp.float32)
    lane = lanes((SLOTS, 128))

    def scores_of(head):
        group = slice((head // 8) * HD, (head // 8 + 1) * HD)
        return lax.dot_general(
            q_ref[:, head * HD : (head + 1) * HD],
            k_ref[:, group],
            (((1,), (1,)), ((), ())),
            preferred_element_type=jnp.float32,
        )

    coming = scores_of(0)
    for head in range(HEADS):
        scores = coming
        if head + 1 < HEADS:
            coming = scores_of(head + 1)
        group = slice((head // 8) * HD, (head // 8 + 1) * HD)
        at = slice(head * HD, (head + 1) * HD)
        top = jnp.max(scores, axis=1, keepdims=True)
        grown = jnp.exp2((scores - top) * (SCALE * LOG2E))
        total = jnp.sum(grown, axis=1, keepdims=True)
        mixed = jnp.dot(
            grown.astype(jnp.bfloat16), v_ref[:, group], preferred_element_type=jnp.float32
        )
        out_ref[:, at] = (mixed / total).astype(jnp.bfloat16)
        logs = jnp.where(lane == head, top * SCALE + jnp.log(total), logs)
    out_ref[:, WIDE:] = split_parts(logs).astype(jnp.bfloat16)


def gather_kernel(back_ref, select_ref, weight_ref, above_ref, below_ref, joined_ref):
    chosen = select_ref[...] > 0.5
    slot_logs = join_parts(back_ref[:, WIDE:].astype(jnp.float32)).T
    lane = lanes((POOL, 128))
    logs = jnp.zeros((POOL, 128), jnp.float32)
    for head in range(HEADS):
        at = slice(head * HD, (head + 1) * HD)
        log = jnp.where(chosen, slot_logs[head : head + 1, :], FAR)
        top = jnp.max(log, axis=1, keepdims=True)
        grown = jnp.where(chosen, jnp.exp(log - top), 0.0)
        total = jnp.maximum(jnp.sum(grown, axis=1, keepdims=True), 0.5)
        weight = grown / total
        high = weight.astype(jnp.bfloat16)
        low = (weight - high.astype(jnp.float32)).astype(jnp.bfloat16)
        mixed = jnp.dot(high, back_ref[:, at], preferred_element_type=jnp.float32)
        mixed = mixed + jnp.dot(low, back_ref[:, at], preferred_element_type=jnp.float32)
        joined_ref[:, at] = mixed.astype(jnp.bfloat16)
        logs = jnp.where(lane == head, top + jnp.log(total), logs)
    joined_ref[:, WIDE:] = split_parts(logs).astype(jnp.bfloat16)


def merge(terms):
    top = terms[0][1]
    for _, log in terms[1:]:
        top = jnp.maximum(top, log)
    lane = lanes((ROWS, 128))
    weights = [jnp.exp(log - top) for _, log in terms]
    total = weights[0]
    for weight in weights[1:]:
        total = total + weight
    columns = []
    for head in range(HEADS):
        at = slice(head * HD, (head + 1) * HD)
        row = None
        for (rows, _), weight in zip(terms, weights):
            term = weight[:, head : head + 1] * rows(at)
            row = term if row is None else row + term
        columns.append(row / total[:, head : head + 1])
    return columns, jnp.where(lane < HEADS, top + jnp.log(total), 0.0)


def packed_term(ref, index):
    rows = slice(index * ROWS, (index + 1) * ROWS)
    return (
        lambda at: ref[rows, at].astype(jnp.float32),
        join_parts(ref[rows, WIDE:].astype(jnp.float32)),
    )


def final_kernel(far_ref, own_ref, own_log_ref, weight_ref, out_ref):
    terms = [packed_term(far_ref, index) for index in range(ZH)]
    terms.append((lambda at: own_ref[:, at], own_log_ref[...]))
    columns, _ = merge(terms)
    for head in range(HEADS):
        rows = columns[head].astype(jnp.bfloat16)
        for copy in range(ZH * ZP):
            out_ref[copy, :, head * HD : (head + 1) * HD] = rows


def project_kernel(rows_ref, *refs):
    out_ref = refs[4]
    for piece in range(4):
        terms = lax.dot_general(
            refs[piece][...], rows_ref[...], (((1,), (1,)), ((), ())), preferred_element_type=jnp.float32
        ).astype(jnp.bfloat16)
        for owner in range(YS):
            for part in range(XS):
                first = (owner * XS + part) * 16
                out_ref[part, piece * YS + owner] = terms[first : first + 16, :]


def sum_kernel(place_ref, terms_ref, out_ref):
    for far_side in range(ZQ):
        side = place_ref[0] if far_side == 0 else 1 - place_ref[0]
        for far_core in range(CS):
            core = place_ref[2] if far_core == 0 else 1 - place_ref[2]
            for order, step in enumerate((0, 1, 3, 2)):
                y = lax.rem(place_ref[1] + step, YS)
                index = (far_side * CS + far_core) * YS + order
                term = terms_ref[0, index].astype(jnp.float32)
                for part in range(1, XS):
                    term = term + terms_ref[part, index].astype(jnp.float32)
                out_ref[(side * YS + y) * CS + core] = term.astype(jnp.bfloat16)


def settle_kernel(place_ref, parts_ref, out_ref):
    lane = lanes((16, 128))
    for side in range(ZQ):
        parts = [
            parts_ref[side * YS * CS + owner].astype(jnp.float32) for owner in range(YS * CS)
        ]
        for far in range(ZH * ZP):
            tile = jnp.zeros((16, 128), jnp.float32)
            for owner in range(YS * CS):
                shift = (owner - far) * ROWS % 128
                moved = parts[owner] if shift == 0 else pltpu.roll(parts[owner], shift, 1)
                tile = jnp.where(lane // ROWS == owner, moved, tile)
            start = (far * ZQ + side) * 128
            out_ref[:, start : start + 128] = tile.astype(jnp.bfloat16)


def own_partials(queries, own_keys, own_values, lengths):
    req_rows, q_heads, head_dim = queries.shape
    kv_heads = own_keys.shape[2]
    grouped = queries.reshape(req_rows, kv_heads, q_heads // kv_heads, head_dim)
    scores = jnp.einsum(
        "rhgd,rlhd->rhgl", grouped, own_keys, preferred_element_type=jnp.float32
    ) * head_dim ** (-0.5)
    visible = jnp.arange(own_keys.shape[1])[None, None, None, :] < lengths[:, None, None, None]
    scores = jnp.where(visible, scores, jnp.float32(-1e30))
    row_top = jnp.max(scores, axis=-1)
    exponent = jnp.exp(scores - row_top[..., None])
    row_total = jnp.sum(exponent, axis=-1)
    weights = exponent.astype(jnp.bfloat16)
    mixed_out = (
        jnp.einsum("rhgl,rlhd->rhgd", weights, own_values, preferred_element_type=jnp.float32)
        / row_total[..., None]
    )
    return (
        mixed_out.reshape(req_rows, q_heads * head_dim),
        (row_top + jnp.log(row_total)).reshape(req_rows, q_heads),
    )


def packed(rows):
    return jax.ShapeDtypeStruct((rows, PACK), jnp.bfloat16)


def inputs(near, far):
    return [pl.BlockSpec(memory_space=pltpu.VMEM)] * near + [
        pl.BlockSpec(memory_space=pl.ANY)
    ] * far


def exchange(value, axis):
    return lax.all_to_all(value, axis, split_axis=0, concat_axis=0, tiled=True)


def on_device(
    queries,
    prefix_keys,
    prefix_values,
    suffix_keys,
    suffix_values,
    out_weight,
    prefix_lists,
    suffix_lengths,
    block_place,
):
    quad = ("zp", "zq", "y", "c")
    swap = [(0, 1), (1, 0)]
    pool = exchange(
        pl.pallas_call(
            prepare_kernel,
            out_shape=jax.ShapeDtypeStruct((ZH, ROWS, PACK), jnp.bfloat16),
            compiler_params=PARAMS,
            name="prepare",
        )(queries, prefix_lists.T),
        "zh",
    ).reshape(POOL, PACK)

    up = [(place, (place + 1) % YS) for place in range(YS)]
    down = [(place, (place - 1) % YS) for place in range(YS)]

    def beside(block):
        return lax.ppermute(block, "y", down), lax.ppermute(block, "y", up)

    def piece_of(block, above, below):
        across = [lax.ppermute(above[:32], "y", down), lax.ppermute(below[32:], "y", up)]
        return jnp.concatenate([block, above, below] + across, axis=0)

    turned = out_weight.T
    facing = lax.ppermute(turned, "zq", swap)
    above, below = beside(turned)
    mine = piece_of(turned, above, below)
    above_far, below_far = beside(facing)
    mine_far = piece_of(facing, above_far, below_far)
    other = lax.ppermute(mine, "c", swap)
    other_far = lax.ppermute(mine_far, "c", swap)
    own_out, own_log = own_partials(queries, suffix_keys, suffix_values, suffix_lengths)

    lane = jnp.arange(128)
    stored = lax.axis_index("zh") * QUAD + lane
    here = (block_place[None, :] == stored[:, None]) & (lane < QUAD)[:, None]
    logical = jnp.sum(jnp.where(here, lane[None, :], 0), axis=1)
    logical = jnp.where(lane < QUAD, logical, -1).astype(jnp.float32)

    outgoing, select = pl.pallas_call(
        dispatch_kernel,
        in_specs=inputs(2, 2),
        out_shape=(
            jax.ShapeDtypeStruct((SLOTS, WIDE), jnp.bfloat16),
            jax.ShapeDtypeStruct((POOL, SLOTS), jnp.float32),
        ),
        compiler_params=PARAMS,
        name="dispatch",
    )(jnp.broadcast_to(logical[None], (8, 128)), pool, above, below)
    arrived = exchange(outgoing, quad)
    partials = pl.pallas_call(
        attend_kernel,
        in_specs=inputs(3, 3),
        out_shape=packed(SLOTS),
        compiler_params=PARAMS,
        name="attend",
    )(
        arrived,
        prefix_keys.reshape(TOKENS, 2 * HD),
        prefix_values.reshape(TOKENS, 2 * HD),
        mine,
        facing,
        own_out,
    )
    back = exchange(partials, quad)
    joined = pl.pallas_call(
        gather_kernel,
        in_specs=inputs(2, 3),
        out_shape=packed(POOL),
        compiler_params=PARAMS,
        name="gather",
    )(back, select, other, above_far, below_far)
    far = exchange(joined, "zh")

    attended = pl.pallas_call(
        final_kernel,
        in_specs=inputs(3, 1),
        out_shape=jax.ShapeDtypeStruct((ZH * ZP, ROWS, WIDE), jnp.bfloat16),
        compiler_params=PARAMS,
        name="final",
    )(far, own_out, jnp.pad(own_log, ((0, 0), (0, 112))), mine_far)

    rows = exchange(attended, ("zh", "zp")).reshape(ZP * POOL, WIDE)
    terms = pl.pallas_call(
        project_kernel,
        out_shape=jax.ShapeDtypeStruct((XS, GROUP, 16, ZP * POOL), jnp.bfloat16),
        compiler_params=PARAMS,
        name="project",
    )(rows, mine, other, mine_far, other_far)
    terms = exchange(terms, "kv")
    place = jnp.stack([lax.axis_index(axis) for axis in ("zq", "y", "c")]).astype(jnp.int32)
    parts = pl.pallas_call(
        sum_kernel,
        in_specs=[
            pl.BlockSpec(memory_space=pltpu.SMEM),
            pl.BlockSpec(memory_space=pltpu.VMEM),
        ],
        out_shape=jax.ShapeDtypeStruct((GROUP, 16, ZP * POOL), jnp.bfloat16),
        compiler_params=PARAMS,
        name="sum",
    )(place, terms)
    parts = exchange(parts, ("zq", "y", "c"))
    return pl.pallas_call(
        settle_kernel,
        in_specs=[
            pl.BlockSpec(memory_space=pltpu.SMEM),
            pl.BlockSpec(memory_space=pltpu.VMEM),
        ],
        out_shape=jax.ShapeDtypeStruct((16, ZH * QUAD * ROWS), jnp.bfloat16),
        compiler_params=PARAMS,
        name="settle",
    )(lax.axis_index("zp").reshape(1).astype(jnp.int32), parts).T


def solution(mesh):
    blk = ("zh", "zp", "zq", "y", "c")
    fine = Mesh(mesh.devices.reshape(ZH, ZP, ZQ, YS, CS, XS), blk + ("kv",))
    placed = (
        P(blk, "kv", None),
        P(blk, None, "kv", None),
        P(blk, None, "kv", None),
        P(blk, None, "kv", None),
        P(blk, None, "kv", None),
        P("kv", blk),
        P(blk, None),
        P(blk),
        P(),
    )
    return jax.shard_map(
        on_device, mesh=fine, in_specs=placed, out_specs=P(None, blk + ("kv",)), check_vma=False
    )
```

```python
import jax
import jax.numpy as jnp
from jax import lax
from jax.experimental import pallas as pl
from jax.experimental.pallas import tpu as pltpu
from jax.sharding import Mesh, PartitionSpec as P

ZH, ZP, ZQ, YS, CS, XS = 4, 2, 2, 4, 2, 4
QUAD = ZP * ZQ * YS * CS
GROUP = ZQ * YS * CS
ROWS = 16
HEADS = 16
HD = 128
WIDE = HEADS * HD
PACK = WIDE + 128
POOL = ZH * ROWS
CAP = 2 * ZH
SLOTS = QUAD * CAP
TOKENS = 1024
FAR = -1e30
SCALE = HD ** -0.5
LOG2E = 1.4426950408889634
PARAMS = pltpu.CompilerParams(vmem_limit_bytes=20 * 1024 * 1024)


def lanes(shape):
    return lax.broadcasted_iota(jnp.int32, shape, len(shape) - 1)


def split_parts(value):
    high = value.astype(jnp.bfloat16).astype(jnp.float32)
    rest = value - high
    middle = rest.astype(jnp.bfloat16).astype(jnp.float32)
    low = (rest - middle).astype(jnp.bfloat16).astype(jnp.float32)
    return high + pltpu.roll(middle, 16, 1) + pltpu.roll(low, 32, 1)


def join_parts(packed):
    whole = packed + pltpu.roll(packed, 112, 1) + pltpu.roll(packed, 96, 1)
    return jnp.where(lanes(whole.shape) < HEADS, whole, 0.0)


def prepare_kernel(queries_ref, listed_ref, out_ref):
    place = lax.broadcasted_iota(jnp.int32, (8, 128), 0)
    spread = jnp.where(lanes((8, 128)) == place, 1.0, 0.0).astype(jnp.bfloat16)
    listed = lax.dot_general(
        listed_ref[...].astype(jnp.float32).astype(jnp.bfloat16),
        spread,
        (((0,), (0,)), ((), ())),
        preferred_element_type=jnp.float32,
    ).astype(jnp.bfloat16)
    heads = [queries_ref[:, head, :] for head in range(HEADS)]
    for copy in range(ZH):
        for head in range(HEADS):
            out_ref[copy, :, head * HD : (head + 1) * HD] = heads[head]
        out_ref[copy, :, WIDE:] = listed


def dispatch_kernel(logical_ref, pool_ref, above_ref, below_ref, out_ref, select_ref):
    listed = pool_ref[:, WIDE:].astype(jnp.float32)
    logical = logical_ref[0:1, :]
    hot = jnp.zeros((POOL, 128), jnp.float32)
    for item in range(8):
        hot = jnp.where(listed[:, item : item + 1] == logical, 1.0, hot)
    hot = hot.astype(jnp.bfloat16)
    row = lax.broadcasted_iota(jnp.int32, (POOL, POOL), 0)
    column = lax.broadcasted_iota(jnp.int32, (POOL, POOL), 1)
    earlier = jnp.where(row > column, 1.0, 0.0).astype(jnp.bfloat16)
    rank = jnp.dot(earlier, hot, preferred_element_type=jnp.float32).astype(jnp.bfloat16)
    owner = lax.broadcasted_iota(jnp.int32, (128, SLOTS), 0)
    slot = lax.broadcasted_iota(jnp.int32, (128, SLOTS), 1)
    spread = jnp.where(slot // CAP == owner, 1.0, 0.0).astype(jnp.bfloat16)
    hot_at = jnp.dot(hot, spread, preferred_element_type=jnp.float32)
    rank_at = jnp.dot(rank, spread, preferred_element_type=jnp.float32)
    wanted = (lanes((POOL, SLOTS)) % CAP).astype(jnp.float32)
    select = jnp.where((hot_at > 0.5) & (rank_at == wanted), 1.0, 0.0)
    select_ref[...] = select
    out_ref[...] = lax.dot_general(
        select.astype(jnp.bfloat16),
        pool_ref[:, :WIDE],
        (((0,), (0,)), ((), ())),
        preferred_element_type=jnp.float32,
    ).astype(jnp.bfloat16)


def attend_kernel(q_ref, keys_ref, values_ref, weight_ref, facing_ref, own_ref, out_ref, k_ref, v_ref, sems):
    copies = []
    for index in range(4):
        source, held = ((keys_ref, k_ref), (values_ref, v_ref))[index % 2]
        group = index // 2
        copy = pltpu.make_async_copy(
            source.at[:, pl.ds(group * HD, HD)], held.at[group], sems.at[index]
        )
        copy.start()
        copies.append(copy)
    logs = jnp.zeros((SLOTS, 128), jnp.float32)
    lane = lanes((SLOTS, 128))

    def scores_of(head):
        if head % 8 == 0:
            copies[head // 8 * 2].wait()
        return lax.dot_general(
            q_ref[:, head * HD : (head + 1) * HD],
            k_ref[head // 8],
            (((1,), (1,)), ((), ())),
            preferred_element_type=jnp.float32,
        )

    coming = scores_of(0)
    for head in range(HEADS):
        scores = coming
        if head + 1 < HEADS:
            coming = scores_of(head + 1)
        if head % 8 == 0:
            copies[head // 8 * 2 + 1].wait()
        at = slice(head * HD, (head + 1) * HD)
        top = jnp.max(scores, axis=1, keepdims=True)
        grown = jnp.exp2((scores - top) * (SCALE * LOG2E))
        total = jnp.sum(grown, axis=1, keepdims=True)
        mixed = jnp.dot(
            grown.astype(jnp.bfloat16), v_ref[head // 8], preferred_element_type=jnp.float32
        )
        out_ref[:, at] = (mixed / total).astype(jnp.bfloat16)
        logs = jnp.where(lane == head, top * SCALE + jnp.log(total), logs)
    out_ref[:, WIDE:] = split_parts(logs).astype(jnp.bfloat16)


def gather_kernel(back_ref, select_ref, weight_ref, above_ref, below_ref, joined_ref):
    chosen = select_ref[...] > 0.5
    slot_logs = join_parts(back_ref[:, WIDE:].astype(jnp.float32)).T
    lane = lanes((POOL, 128))
    logs = jnp.zeros((POOL, 128), jnp.float32)
    for head in range(HEADS):
        at = slice(head * HD, (head + 1) * HD)
        log = jnp.where(chosen, slot_logs[head : head + 1, :], FAR)
        top = jnp.max(log, axis=1, keepdims=True)
        grown = jnp.where(chosen, jnp.exp(log - top), 0.0)
        total = jnp.maximum(jnp.sum(grown, axis=1, keepdims=True), 0.5)
        weight = grown / total
        high = weight.astype(jnp.bfloat16)
        low = (weight - high.astype(jnp.float32)).astype(jnp.bfloat16)
        mixed = jnp.dot(high, back_ref[:, at], preferred_element_type=jnp.float32)
        mixed = mixed + jnp.dot(low, back_ref[:, at], preferred_element_type=jnp.float32)
        joined_ref[:, at] = mixed.astype(jnp.bfloat16)
        logs = jnp.where(lane == head, top + jnp.log(total), logs)
    joined_ref[:, WIDE:] = split_parts(logs).astype(jnp.bfloat16)


def merge(terms):
    top = terms[0][1]
    for _, log in terms[1:]:
        top = jnp.maximum(top, log)
    lane = lanes((ROWS, 128))
    weights = [jnp.exp(log - top) for _, log in terms]
    total = weights[0]
    for weight in weights[1:]:
        total = total + weight
    columns = []
    for head in range(HEADS):
        at = slice(head * HD, (head + 1) * HD)
        row = None
        for (rows, _), weight in zip(terms, weights):
            term = weight[:, head : head + 1] * rows(at)
            row = term if row is None else row + term
        columns.append(row / total[:, head : head + 1])
    return columns, jnp.where(lane < HEADS, top + jnp.log(total), 0.0)


def packed_term(ref, index):
    rows = slice(index * ROWS, (index + 1) * ROWS)
    return (
        lambda at: ref[rows, at].astype(jnp.float32),
        join_parts(ref[rows, WIDE:].astype(jnp.float32)),
    )


def final_kernel(far_ref, own_ref, own_log_ref, weight_ref, out_ref):
    terms = [packed_term(far_ref, index) for index in range(ZH)]
    terms.append((lambda at: own_ref[:, at], own_log_ref[...]))
    columns, _ = merge(terms)
    for head in range(HEADS):
        rows = columns[head].astype(jnp.bfloat16)
        for copy in range(ZH * ZP):
            out_ref[copy, :, head * HD : (head + 1) * HD] = rows


def project_kernel(place_ref, rows_ref, *refs):
    sources, out_ref, held, sems = refs[:4], refs[4], refs[5], refs[6]
    half_rows = YS * 64 // 2
    copies = []
    for piece, source in enumerate(sources):
        for half in range(2):
            rows = pl.ds(half * half_rows, half_rows)
            copy = pltpu.make_async_copy(
                source.at[rows, :], held.at[piece, rows, :], sems.at[piece * 2 + half]
            )
            copy.start()
            copies.append(copy)
    for piece in range(4):
        far_side, far_core = divmod(piece, CS)
        side = place_ref[0] if far_side == 0 else 1 - place_ref[0]
        core = place_ref[2] if far_core == 0 else 1 - place_ref[2]
        for half, steps in enumerate(((0, 1), (3, 2))):
            copies[piece * 2 + half].wait()
            terms = lax.dot_general(
                held[piece, half * half_rows : (half + 1) * half_rows, :],
                rows_ref[...],
                (((1,), (1,)), ((), ())),
                preferred_element_type=jnp.float32,
            ).astype(jnp.bfloat16)
            for index, step in enumerate(steps):
                owner = (side * YS + lax.rem(place_ref[1] + step, YS)) * CS + core
                for part in range(XS):
                    first = (index * XS + part) * 16
                    out_ref[owner * XS + part] = terms[first : first + 16, :]


def settle_kernel(terms_ref, out_ref):
    lane = lanes((16, 128))
    for side in range(ZQ):
        parts = []
        for owner in range(YS * CS):
            first = (side * YS * CS + owner) * XS
            term = terms_ref[first].astype(jnp.float32)
            for part in range(1, XS):
                term = term + terms_ref[first + part].astype(jnp.float32)
            parts.append(term)
        for far in range(ZH * ZP):
            tile = jnp.zeros((16, 128), jnp.float32)
            for owner in range(YS * CS):
                shift = (owner - far) * ROWS % 128
                moved = parts[owner] if shift == 0 else pltpu.roll(parts[owner], shift, 1)
                tile = jnp.where(lane // ROWS == owner, moved, tile)
            start = (far * ZQ + side) * 128
            out_ref[:, start : start + 128] = tile.astype(jnp.bfloat16)


def own_partials(queries, own_keys, own_values, lengths):
    req_rows, q_heads, head_dim = queries.shape
    kv_heads = own_keys.shape[2]
    grouped = queries.reshape(req_rows, kv_heads, q_heads // kv_heads, head_dim)
    scores = jnp.einsum(
        "rhgd,rlhd->rhgl", grouped, own_keys, preferred_element_type=jnp.float32
    ) * head_dim ** (-0.5)
    visible = jnp.arange(own_keys.shape[1])[None, None, None, :] < lengths[:, None, None, None]
    scores = jnp.where(visible, scores, jnp.float32(-1e30))
    row_top = jnp.max(scores, axis=-1)
    exponent = jnp.exp(scores - row_top[..., None])
    row_total = jnp.sum(exponent, axis=-1)
    weights = exponent.astype(jnp.bfloat16)
    mixed_out = (
        jnp.einsum("rhgl,rlhd->rhgd", weights, own_values, preferred_element_type=jnp.float32)
        / row_total[..., None]
    )
    return (
        mixed_out.reshape(req_rows, q_heads * head_dim),
        (row_top + jnp.log(row_total)).reshape(req_rows, q_heads),
    )


def packed(rows):
    return jax.ShapeDtypeStruct((rows, PACK), jnp.bfloat16)


def inputs(near, far):
    return [pl.BlockSpec(memory_space=pltpu.VMEM)] * near + [
        pl.BlockSpec(memory_space=pl.ANY)
    ] * far


def exchange(value, axis):
    return lax.all_to_all(value, axis, split_axis=0, concat_axis=0, tiled=True)


def on_device(
    queries,
    prefix_keys,
    prefix_values,
    suffix_keys,
    suffix_values,
    out_weight,
    prefix_lists,
    suffix_lengths,
    block_place,
):
    quad = ("zp", "zq", "y", "c")
    swap = [(0, 1), (1, 0)]
    pool = exchange(
        pl.pallas_call(
            prepare_kernel,
            out_shape=jax.ShapeDtypeStruct((ZH, ROWS, PACK), jnp.bfloat16),
            compiler_params=PARAMS,
            name="prepare",
        )(queries, prefix_lists.T),
        "zh",
    ).reshape(POOL, PACK)

    up = [(place, (place + 1) % YS) for place in range(YS)]
    down = [(place, (place - 1) % YS) for place in range(YS)]

    def beside(block):
        return lax.ppermute(block, "y", down), lax.ppermute(block, "y", up)

    def piece_of(block, above, below):
        across = [lax.ppermute(above[:32], "y", down), lax.ppermute(below[32:], "y", up)]
        return jnp.concatenate([block, above, below] + across, axis=0)

    turned = out_weight.T
    facing = lax.ppermute(turned, "zq", swap)
    above, below = beside(turned)
    mine = piece_of(turned, above, below)
    above_far, below_far = beside(facing)
    mine_far = piece_of(facing, above_far, below_far)
    other = lax.ppermute(mine, "c", swap)
    other_far = lax.ppermute(mine_far, "c", swap)
    own_out, own_log = own_partials(queries, suffix_keys, suffix_values, suffix_lengths)

    lane = jnp.arange(128)
    stored = lax.axis_index("zh") * QUAD + lane
    here = (block_place[None, :] == stored[:, None]) & (lane < QUAD)[:, None]
    logical = jnp.sum(jnp.where(here, lane[None, :], 0), axis=1)
    logical = jnp.where(lane < QUAD, logical, -1).astype(jnp.float32)

    outgoing, select = pl.pallas_call(
        dispatch_kernel,
        in_specs=inputs(2, 2),
        out_shape=(
            jax.ShapeDtypeStruct((SLOTS, WIDE), jnp.bfloat16),
            jax.ShapeDtypeStruct((POOL, SLOTS), jnp.float32),
        ),
        compiler_params=PARAMS,
        name="dispatch",
    )(jnp.broadcast_to(logical[None], (8, 128)), pool, above, below)
    arrived = exchange(outgoing, quad)
    partials = pl.pallas_call(
        attend_kernel,
        in_specs=[pl.BlockSpec(memory_space=pltpu.VMEM)]
        + [pl.BlockSpec(memory_space=pltpu.HBM)] * 2
        + [pl.BlockSpec(memory_space=pl.ANY)] * 3,
        out_shape=packed(SLOTS),
        scratch_shapes=[
            pltpu.VMEM((2, TOKENS, HD), jnp.bfloat16),
            pltpu.VMEM((2, TOKENS, HD), jnp.bfloat16),
            pltpu.SemaphoreType.DMA((4,)),
        ],
        compiler_params=PARAMS,
        name="attend",
    )(
        arrived,
        prefix_keys.reshape(TOKENS, 2 * HD),
        prefix_values.reshape(TOKENS, 2 * HD),
        mine,
        facing,
        own_out,
    )
    back = exchange(partials, quad)
    joined = pl.pallas_call(
        gather_kernel,
        in_specs=inputs(2, 3),
        out_shape=packed(POOL),
        compiler_params=PARAMS,
        name="gather",
    )(back, select, other, above_far, below_far)
    far = exchange(joined, "zh")

    attended = pl.pallas_call(
        final_kernel,
        in_specs=inputs(3, 1),
        out_shape=jax.ShapeDtypeStruct((ZH * ZP, ROWS, WIDE), jnp.bfloat16),
        compiler_params=PARAMS,
        name="final",
    )(far, own_out, jnp.pad(own_log, ((0, 0), (0, 112))), mine_far)

    rows = exchange(attended, ("zh", "zp")).reshape(ZP * POOL, WIDE)
    owners = ("zq", "y", "c")
    terms = pl.pallas_call(
        project_kernel,
        in_specs=[pl.BlockSpec(memory_space=pltpu.SMEM), pl.BlockSpec(memory_space=pltpu.VMEM)]
        + [pl.BlockSpec(memory_space=pltpu.HBM)] * 4,
        out_shape=jax.ShapeDtypeStruct((GROUP * XS, 16, ZP * POOL), jnp.bfloat16),
        scratch_shapes=[
            pltpu.VMEM((4, YS * 64, WIDE), jnp.bfloat16),
            pltpu.SemaphoreType.DMA((8,)),
        ],
        compiler_params=PARAMS,
        name="project",
    )(
        jnp.stack([lax.axis_index(axis) for axis in owners]).astype(jnp.int32),
        rows,
        mine,
        other,
        mine_far,
        other_far,
    )
    return pl.pallas_call(
        settle_kernel,
        out_shape=jax.ShapeDtypeStruct((16, ZH * QUAD * ROWS), jnp.bfloat16),
        compiler_params=PARAMS,
        name="settle",
    )(exchange(terms, owners + ("kv",))).T


def solution(mesh):
    blk = ("zh", "zp", "zq", "y", "c")
    fine = Mesh(mesh.devices.reshape(ZH, ZP, ZQ, YS, CS, XS), blk + ("kv",))
    placed = (
        P(blk, "kv", None),
        P(blk, None, "kv", None),
        P(blk, None, "kv", None),
        P(blk, None, "kv", None),
        P(blk, None, "kv", None),
        P("kv", blk),
        P(blk, None),
        P(blk),
        P(),
    )
    return jax.shard_map(
        on_device, mesh=fine, in_specs=placed, out_specs=P(None, blk + ("kv",)), check_vma=False
    )
```

```python
import jax
import jax.numpy as jnp
from jax import lax
from jax.experimental import pallas as pl
from jax.experimental.pallas import tpu as pltpu
from jax.sharding import Mesh, PartitionSpec as P

ZH, ZP, ZQ, YS, CS, XS = 4, 2, 2, 4, 2, 4
QUAD = ZP * ZQ * YS * CS
GROUP = ZQ * YS * CS
ROWS = 16
HEADS = 16
HD = 128
WIDE = HEADS * HD
PACK = WIDE + 128
POOL = ZH * ROWS
CAP = 2 * ZH
SLOTS = QUAD * CAP
TOKENS = 1024
FAR = -1e30
SCALE = HD ** -0.5
LOG2E = 1.4426950408889634
PARAMS = pltpu.CompilerParams(vmem_limit_bytes=20 * 1024 * 1024)


def lanes(shape):
    return lax.broadcasted_iota(jnp.int32, shape, len(shape) - 1)


def split_parts(value):
    high = value.astype(jnp.bfloat16).astype(jnp.float32)
    rest = value - high
    middle = rest.astype(jnp.bfloat16).astype(jnp.float32)
    low = (rest - middle).astype(jnp.bfloat16).astype(jnp.float32)
    return high + pltpu.roll(middle, 16, 1) + pltpu.roll(low, 32, 1)


def join_parts(packed):
    whole = packed + pltpu.roll(packed, 112, 1) + pltpu.roll(packed, 96, 1)
    return jnp.where(lanes(whole.shape) < HEADS, whole, 0.0)


def prepare_kernel(queries_ref, listed_ref, out_ref):
    place = lax.broadcasted_iota(jnp.int32, (8, 128), 0)
    spread = jnp.where(lanes((8, 128)) == place, 1.0, 0.0).astype(jnp.bfloat16)
    listed = lax.dot_general(
        listed_ref[...].astype(jnp.float32).astype(jnp.bfloat16),
        spread,
        (((0,), (0,)), ((), ())),
        preferred_element_type=jnp.float32,
    ).astype(jnp.bfloat16)
    heads = [queries_ref[:, head, :] for head in range(HEADS)]
    for copy in range(ZH):
        for head in range(HEADS):
            out_ref[copy, :, head * HD : (head + 1) * HD] = heads[head]
        out_ref[copy, :, WIDE:] = listed


def dispatch_kernel(logical_ref, pool_ref, above_ref, below_ref, out_ref, select_ref):
    listed = pool_ref[:, WIDE:].astype(jnp.float32)
    logical = logical_ref[0:1, :]
    hot = jnp.zeros((POOL, 128), jnp.float32)
    for item in range(8):
        hot = jnp.where(listed[:, item : item + 1] == logical, 1.0, hot)
    hot = hot.astype(jnp.bfloat16)
    row = lax.broadcasted_iota(jnp.int32, (POOL, POOL), 0)
    column = lax.broadcasted_iota(jnp.int32, (POOL, POOL), 1)
    earlier = jnp.where(row > column, 1.0, 0.0).astype(jnp.bfloat16)
    rank = jnp.dot(earlier, hot, preferred_element_type=jnp.float32).astype(jnp.bfloat16)
    owner = lax.broadcasted_iota(jnp.int32, (128, SLOTS), 0)
    slot = lax.broadcasted_iota(jnp.int32, (128, SLOTS), 1)
    spread = jnp.where(slot // CAP == owner, 1.0, 0.0).astype(jnp.bfloat16)
    hot_at = jnp.dot(hot, spread, preferred_element_type=jnp.float32)
    rank_at = jnp.dot(rank, spread, preferred_element_type=jnp.float32)
    wanted = (lanes((POOL, SLOTS)) % CAP).astype(jnp.float32)
    select = jnp.where((hot_at > 0.5) & (rank_at == wanted), 1.0, 0.0)
    select_ref[...] = select
    out_ref[...] = lax.dot_general(
        select.astype(jnp.bfloat16),
        pool_ref[:, :WIDE],
        (((0,), (0,)), ((), ())),
        preferred_element_type=jnp.float32,
    ).astype(jnp.bfloat16)


def attend_kernel(q_ref, k_ref, v_ref, weight_ref, facing_ref, own_ref, out_ref):
    logs = jnp.zeros((SLOTS, 128), jnp.float32)
    lane = lanes((SLOTS, 128))

    def scores_of(head):
        group = slice((head // 8) * HD, (head // 8 + 1) * HD)
        return lax.dot_general(
            q_ref[:, head * HD : (head + 1) * HD],
            k_ref[:, group],
            (((1,), (1,)), ((), ())),
            preferred_element_type=jnp.float32,
        )

    coming = scores_of(0)
    for head in range(HEADS):
        scores = coming
        if head + 1 < HEADS:
            coming = scores_of(head + 1)
        group = slice((head // 8) * HD, (head // 8 + 1) * HD)
        at = slice(head * HD, (head + 1) * HD)
        top = jnp.max(scores, axis=1, keepdims=True)
        grown = jnp.exp2((scores - top) * (SCALE * LOG2E))
        total = jnp.sum(grown, axis=1, keepdims=True)
        mixed = jnp.dot(
            grown.astype(jnp.bfloat16), v_ref[:, group], preferred_element_type=jnp.float32
        )
        out_ref[:, at] = (mixed / total).astype(jnp.bfloat16)
        logs = jnp.where(lane == head, top * SCALE + jnp.log(total), logs)
    out_ref[:, WIDE:] = split_parts(logs).astype(jnp.bfloat16)


def gather_kernel(back_ref, select_ref, weight_ref, above_ref, below_ref, joined_ref):
    chosen = select_ref[...] > 0.5
    slot_logs = join_parts(back_ref[:, WIDE:].astype(jnp.float32)).T
    lane = lanes((POOL, 128))
    logs = jnp.zeros((POOL, 128), jnp.float32)
    for head in range(HEADS):
        at = slice(head * HD, (head + 1) * HD)
        log = jnp.where(chosen, slot_logs[head : head + 1, :], FAR)
        top = jnp.max(log, axis=1, keepdims=True)
        grown = jnp.where(chosen, jnp.exp(log - top), 0.0)
        total = jnp.maximum(jnp.sum(grown, axis=1, keepdims=True), 0.5)
        weight = grown / total
        high = weight.astype(jnp.bfloat16)
        low = (weight - high.astype(jnp.float32)).astype(jnp.bfloat16)
        mixed = jnp.dot(high, back_ref[:, at], preferred_element_type=jnp.float32)
        mixed = mixed + jnp.dot(low, back_ref[:, at], preferred_element_type=jnp.float32)
        joined_ref[:, at] = mixed.astype(jnp.bfloat16)
        logs = jnp.where(lane == head, top + jnp.log(total), logs)
    joined_ref[:, WIDE:] = split_parts(logs).astype(jnp.bfloat16)


def merge(terms):
    top = terms[0][1]
    for _, log in terms[1:]:
        top = jnp.maximum(top, log)
    lane = lanes((ROWS, 128))
    weights = [jnp.exp(log - top) for _, log in terms]
    total = weights[0]
    for weight in weights[1:]:
        total = total + weight
    columns = []
    for head in range(HEADS):
        at = slice(head * HD, (head + 1) * HD)
        row = None
        for (rows, _), weight in zip(terms, weights):
            term = weight[:, head : head + 1] * rows(at)
            row = term if row is None else row + term
        columns.append(row / total[:, head : head + 1])
    return columns, jnp.where(lane < HEADS, top + jnp.log(total), 0.0)


def packed_term(ref, index):
    rows = slice(index * ROWS, (index + 1) * ROWS)
    return (
        lambda at: ref[rows, at].astype(jnp.float32),
        join_parts(ref[rows, WIDE:].astype(jnp.float32)),
    )


def final_kernel(far_ref, own_ref, own_log_ref, weight_ref, out_ref):
    terms = [packed_term(far_ref, index) for index in range(ZH)]
    terms.append((lambda at: own_ref[:, at], own_log_ref[...]))
    columns, _ = merge(terms)
    for head in range(HEADS):
        rows = columns[head].astype(jnp.bfloat16)
        for copy in range(ZH * ZP):
            out_ref[copy, :, head * HD : (head + 1) * HD] = rows


def project_kernel(place_ref, rows_ref, *refs):
    sources, out_ref, held, sems = refs[:4], refs[4], refs[5], refs[6]
    copies = []
    for piece, source in enumerate(sources):
        copy = pltpu.make_async_copy(source, held.at[piece], sems.at[piece])
        copy.start()
        copies.append(copy)
    for piece in range(4):
        far_side, far_core = divmod(piece, CS)
        side = place_ref[0] if far_side == 0 else 1 - place_ref[0]
        core = place_ref[2] if far_core == 0 else 1 - place_ref[2]
        copies[piece].wait()
        terms = lax.dot_general(
            held[piece], rows_ref[...], (((1,), (1,)), ((), ())), preferred_element_type=jnp.float32
        ).astype(jnp.bfloat16)
        for order, step in enumerate((0, 1, 3, 2)):
            owner = (side * YS + lax.rem(place_ref[1] + step, YS)) * CS + core
            for part in range(XS):
                first = (order * XS + part) * 16
                out_ref[owner * XS + part] = terms[first : first + 16, :]


def settle_kernel(terms_ref, out_ref):
    lane = lanes((16, 128))
    for side in range(ZQ):
        parts = []
        for owner in range(YS * CS):
            first = (side * YS * CS + owner) * XS
            term = terms_ref[first].astype(jnp.float32)
            for part in range(1, XS):
                term = term + terms_ref[first + part].astype(jnp.float32)
            parts.append(term)
        for far in range(ZH * ZP):
            tile = jnp.zeros((16, 128), jnp.float32)
            for owner in range(YS * CS):
                shift = (owner - far) * ROWS % 128
                moved = parts[owner] if shift == 0 else pltpu.roll(parts[owner], shift, 1)
                tile = jnp.where(lane // ROWS == owner, moved, tile)
            start = (far * ZQ + side) * 128
            out_ref[:, start : start + 128] = tile.astype(jnp.bfloat16)


def own_partials(queries, own_keys, own_values, lengths):
    req_rows, q_heads, head_dim = queries.shape
    kv_heads = own_keys.shape[2]
    grouped = queries.reshape(req_rows, kv_heads, q_heads // kv_heads, head_dim)
    scores = jnp.einsum(
        "rhgd,rlhd->rhgl", grouped, own_keys, preferred_element_type=jnp.float32
    ) * head_dim ** (-0.5)
    visible = jnp.arange(own_keys.shape[1])[None, None, None, :] < lengths[:, None, None, None]
    scores = jnp.where(visible, scores, jnp.float32(-1e30))
    row_top = jnp.max(scores, axis=-1)
    exponent = jnp.exp(scores - row_top[..., None])
    row_total = jnp.sum(exponent, axis=-1)
    weights = exponent.astype(jnp.bfloat16)
    mixed_out = (
        jnp.einsum("rhgl,rlhd->rhgd", weights, own_values, preferred_element_type=jnp.float32)
        / row_total[..., None]
    )
    return (
        mixed_out.reshape(req_rows, q_heads * head_dim),
        (row_top + jnp.log(row_total)).reshape(req_rows, q_heads),
    )


def packed(rows):
    return jax.ShapeDtypeStruct((rows, PACK), jnp.bfloat16)


def inputs(near, far):
    return [pl.BlockSpec(memory_space=pltpu.VMEM)] * near + [
        pl.BlockSpec(memory_space=pl.ANY)
    ] * far


def exchange(value, axis):
    return lax.all_to_all(value, axis, split_axis=0, concat_axis=0, tiled=True)


def on_device(
    queries,
    prefix_keys,
    prefix_values,
    suffix_keys,
    suffix_values,
    out_weight,
    prefix_lists,
    suffix_lengths,
    block_place,
):
    quad = ("zp", "zq", "y", "c")
    swap = [(0, 1), (1, 0)]
    pool = exchange(
        pl.pallas_call(
            prepare_kernel,
            out_shape=jax.ShapeDtypeStruct((ZH, ROWS, PACK), jnp.bfloat16),
            compiler_params=PARAMS,
            name="prepare",
        )(queries, prefix_lists.T),
        "zh",
    ).reshape(POOL, PACK)

    up = [(place, (place + 1) % YS) for place in range(YS)]
    down = [(place, (place - 1) % YS) for place in range(YS)]

    def beside(block):
        return lax.ppermute(block, "y", down), lax.ppermute(block, "y", up)

    def piece_of(block, above, below):
        across = [lax.ppermute(above[:32], "y", down), lax.ppermute(below[32:], "y", up)]
        return jnp.concatenate([block, above, below] + across, axis=0)

    turned = out_weight.T
    facing = lax.ppermute(turned, "zq", swap)
    above, below = beside(turned)
    mine = piece_of(turned, above, below)
    above_far, below_far = beside(facing)
    mine_far = piece_of(facing, above_far, below_far)
    other = lax.ppermute(mine, "c", swap)
    other_far = lax.ppermute(mine_far, "c", swap)
    own_out, own_log = own_partials(queries, suffix_keys, suffix_values, suffix_lengths)

    lane = jnp.arange(128)
    stored = lax.axis_index("zh") * QUAD + lane
    here = (block_place[None, :] == stored[:, None]) & (lane < QUAD)[:, None]
    logical = jnp.sum(jnp.where(here, lane[None, :], 0), axis=1)
    logical = jnp.where(lane < QUAD, logical, -1).astype(jnp.float32)

    outgoing, select = pl.pallas_call(
        dispatch_kernel,
        in_specs=inputs(2, 2),
        out_shape=(
            jax.ShapeDtypeStruct((SLOTS, WIDE), jnp.bfloat16),
            jax.ShapeDtypeStruct((POOL, SLOTS), jnp.float32),
        ),
        compiler_params=PARAMS,
        name="dispatch",
    )(jnp.broadcast_to(logical[None], (8, 128)), pool, above, below)
    arrived = exchange(outgoing, quad)
    partials = pl.pallas_call(
        attend_kernel,
        in_specs=inputs(3, 3),
        out_shape=packed(SLOTS),
        compiler_params=PARAMS,
        name="attend",
    )(
        arrived,
        prefix_keys.reshape(TOKENS, 2 * HD),
        prefix_values.reshape(TOKENS, 2 * HD),
        mine,
        facing,
        own_out,
    )
    back = exchange(partials, quad)
    joined = pl.pallas_call(
        gather_kernel,
        in_specs=inputs(2, 3),
        out_shape=packed(POOL),
        compiler_params=PARAMS,
        name="gather",
    )(back, select, other, above_far, below_far)
    far = exchange(joined, "zh")

    attended = pl.pallas_call(
        final_kernel,
        in_specs=inputs(3, 1),
        out_shape=jax.ShapeDtypeStruct((ZH * ZP, ROWS, WIDE), jnp.bfloat16),
        compiler_params=PARAMS,
        name="final",
    )(far, own_out, jnp.pad(own_log, ((0, 0), (0, 112))), mine_far)

    rows = exchange(attended, ("zh", "zp")).reshape(ZP * POOL, WIDE)
    owners = ("zq", "y", "c")
    terms = pl.pallas_call(
        project_kernel,
        in_specs=[pl.BlockSpec(memory_space=pltpu.SMEM), pl.BlockSpec(memory_space=pltpu.VMEM)]
        + [pl.BlockSpec(memory_space=pltpu.HBM)] * 4,
        out_shape=jax.ShapeDtypeStruct((GROUP * XS, 16, ZP * POOL), jnp.bfloat16),
        scratch_shapes=[
            pltpu.VMEM((4, YS * 64, WIDE), jnp.bfloat16),
            pltpu.SemaphoreType.DMA((4,)),
        ],
        compiler_params=PARAMS,
        name="project",
    )(
        jnp.stack([lax.axis_index(axis) for axis in owners]).astype(jnp.int32),
        rows,
        mine,
        other,
        mine_far,
        other_far,
    )
    return pl.pallas_call(
        settle_kernel,
        out_shape=jax.ShapeDtypeStruct((16, ZH * QUAD * ROWS), jnp.bfloat16),
        compiler_params=PARAMS,
        name="settle",
    )(exchange(terms, owners + ("kv",))).T


def solution(mesh):
    blk = ("zh", "zp", "zq", "y", "c")
    fine = Mesh(mesh.devices.reshape(ZH, ZP, ZQ, YS, CS, XS), blk + ("kv",))
    placed = (
        P(blk, "kv", None),
        P(blk, None, "kv", None),
        P(blk, None, "kv", None),
        P(blk, None, "kv", None),
        P(blk, None, "kv", None),
        P("kv", blk),
        P(blk, None),
        P(blk),
        P(),
    )
    return jax.shard_map(
        on_device, mesh=fine, in_specs=placed, out_specs=P(None, blk + ("kv",)), check_vma=False
    )
```
